256 devices in a mesh: img: 32 (over y, x, core), txt: 8 (over z).
Axes of the slice: x: 4, y: 4, z: 8, core: 2. Of those that a mesh axis runs over, the one named last changes fastest.
Arguments:
- image_embed: bfloat16 [12288, 1280], P(('img', 'txt'))
- text_embed: bfloat16 [12288, 1280], P(('txt', 'img'))
- pair_col: int32 [12288], P('img'), may hold values from 0 to 12287, each once
- log_scale: float32 [], replicated, may hold values from 2.303 to 3.912
Outputs:
- row_loss: float32 [12288], P('img')
- col_loss: float32 [12288], P('txt')
- grad_image: float32 [12288, 1280], P(('img', 'txt'))
- grad_text: float32 [12288, 1280], P(('txt', 'img'))
- temp_grad: float32 [], replicated
The draws below stay inside these ranges and needn't reach their ends.
Inputs may be any that keep to these rules, and one draw needn't show every extreme that they name: pair_col is a permutation of the 12288 text indices.
All inputs are finite; a program needn't handle non-finite values.
Results may differ from the reference program's by a relative error of at most 0.003.
Values may be sent and summed in bfloat16 or wider, within the bound.
No kernel may reach another device: no remote copies, remote signals or barrier semaphores. Data moves between devices by JAX's collectives and lax.ppermute only.
A program may use at most 64 MiB of HBM per device.

```python
import math
import jax
import jax.numpy as jnp
from jax import lax

E = 1280
BATCH = 12288


def shared_texts(key):
    return jax.random.normal(key, (BATCH, E), jnp.float32) / jnp.sqrt(jnp.float32(E))


def draw_text_embed(key, part):
    base = shared_texts(key)
    key = jax.random.fold_in(key, 2)
    scale_key = jax.random.fold_in(key, 0)
    scales = jnp.exp(jax.random.uniform(scale_key, (BATCH, 1), jnp.float32, jnp.log(0.3), jnp.log(3.0)))
    values = base * scales
    return values.astype(jnp.bfloat16)


def draw_image_embed(key, part):
    key = jax.random.fold_in(key, 1)
    own_key, scale_key = jax.random.split(key, 2)
    values = jax.random.normal(own_key, (BATCH, E), jnp.float32) / jnp.sqrt(jnp.float32(E))
    scales = jnp.exp(jax.random.uniform(scale_key, (BATCH, 1), jnp.float32, jnp.log(0.3), jnp.log(3.0)))
    values = values * scales
    return values.astype(jnp.bfloat16)


def setup_inputs(seed: int = 0) -> dict:
    streams_of = jax.random.split(jax.random.key(seed), 5)
    image_embed = draw_image_embed(jax.random.fold_in(streams_of[4], 71), 0)
    text_embed = draw_text_embed(jax.random.fold_in(streams_of[4], 71), 0)
    pair_col = jax.random.permutation(streams_of[2], BATCH).astype(jnp.int32)
    log_scale = jnp.clip(jax.random.uniform(streams_of[3], (), jnp.float32, 2.303, 3.912), 2.303, 3.912)
    return {"image_embed": image_embed, "text_embed": text_embed, "pair_col": pair_col, "log_scale": log_scale}


def reference(image_embed, text_embed, pair_col, log_scale):
    scale = jnp.exp(log_scale)
    block = math.gcd(BATCH, 512)
    count = BATCH // block
    img_blocks = image_embed.reshape(count, block, E)
    pair_blocks = pair_col.reshape(count, block)
    columns = jnp.arange(BATCH, dtype=jnp.int32)

    def logits_of(rows_in):
        return scale * jnp.dot(rows_in, text_embed.T, preferred_element_type=jnp.float32)

    def first_pass(carry, item):
        col_max, col_sum, col_pos = carry
        rows_in, pairs = item
        logits = logits_of(rows_in)
        hit = pairs[:, None] == columns[None, :]
        paired = jnp.where(hit, logits, jnp.float32(0.0))
        row_max = jnp.max(logits, axis=1)
        row_sum = jnp.sum(jnp.exp(logits - row_max[:, None]), axis=1)
        row_lse = row_max + jnp.log(row_sum)
        new_max = jnp.maximum(col_max, jnp.max(logits, axis=0))
        col_sum = col_sum * jnp.exp(col_max - new_max) + jnp.sum(jnp.exp(logits - new_max[None, :]), axis=0)
        col_pos = col_pos + jnp.sum(paired, axis=0)
        return (new_max, col_sum, col_pos), (row_lse, jnp.sum(paired, axis=1))

    start = (jnp.full((BATCH,), -jnp.inf, jnp.float32), jnp.zeros((BATCH,), jnp.float32), jnp.zeros((BATCH,), jnp.float32))
    (col_max, col_sum, col_pos), (row_lse, row_pos) = lax.scan(first_pass, start, (img_blocks, pair_blocks))
    col_lse = col_max + jnp.log(col_sum)
    row_loss = (row_lse - row_pos).reshape(BATCH)
    col_loss = col_lse - col_pos

    def second_pass(carry, item):
        grad_text, total = carry
        rows_in, pairs, lse_rows = item
        logits = logits_of(rows_in)
        hit = (pairs[:, None] == columns[None, :]).astype(jnp.float32)
        grad_logits = 0.5 * (jnp.exp(logits - lse_rows[:, None]) + jnp.exp(logits - col_lse[None, :])) - hit
        scaled_grad = (scale * grad_logits).astype(jnp.bfloat16)
        grad_rows = jnp.dot(scaled_grad, text_embed, preferred_element_type=jnp.float32)
        grad_text = grad_text + jnp.dot(scaled_grad.T, rows_in, preferred_element_type=jnp.float32)
        total = total + jnp.sum(grad_logits * logits)
        return (grad_text, total), grad_rows

    start2 = (jnp.zeros((BATCH, E), jnp.float32), jnp.zeros((), jnp.float32))
    (grad_text, total), grad_image = lax.scan(second_pass, start2, (img_blocks, pair_blocks, row_lse))
    grad_image = grad_image.reshape(BATCH, E)
    temp_grad = total / BATCH
    return row_loss, col_loss, grad_image, grad_text, temp_grad
```

```python
import jax
import jax.numpy as jnp
from jax import lax
from jax.sharding import Mesh, PartitionSpec as P

NY, NX, NC = 4, 4, 2
XY = ("y", "x")
CZ = ("c", "z")
SWAP = [(0, 1), (1, 0)]


def merge(lse, mean):
    top = jnp.max(lse, axis=0)
    weight = jnp.exp(lse - top)
    total = jnp.sum(weight, axis=0)
    return top + jnp.log(total), jnp.sum(weight * mean, axis=0) / total


def local(image_embed, text_embed, pair_col, log_scale):
    part, embed = image_embed.shape
    peers = NY * NX
    nz = lax.axis_size("z")
    c = lax.axis_index("c")
    z = lax.axis_index("z")
    scale = jnp.exp(log_scale)

    img = lax.all_gather(image_embed, CZ, axis=0, tiled=True)
    txt = lax.all_to_all(jnp.broadcast_to(text_embed[None], (peers, part, embed)), XY, 0, 0)
    txt = txt.reshape(peers * part, embed)
    rows, cols = img.shape[0], txt.shape[0]
    pairs = lax.all_gather(pair_col, "c", axis=0, tiled=True)
    k = jnp.arange(cols, dtype=jnp.int32)
    col_ids = z * (peers * NC * part) + (2 * (k // part) + c) * part + k % part
    hit = pairs[:, None] == col_ids[None, :]

    logits = scale * lax.dot_general(
        img, txt, (((1,), (1,)), ((), ())), preferred_element_type=jnp.float32
    )
    paired = jnp.where(hit, logits, jnp.float32(0.0))
    row_part = jnp.sum(paired, axis=1)
    col_part = jnp.sum(paired, axis=0)
    row_top = jnp.max(logits, axis=1)
    col_top = jnp.max(logits, axis=0)
    row_exp = jnp.exp(logits - row_top[:, None])
    col_exp = jnp.exp(logits - col_top[None, :])
    row_sum = jnp.sum(row_exp, axis=1)
    col_sum = jnp.sum(col_exp, axis=0)
    row_mean = jnp.sum(row_exp * logits, axis=1) / row_sum
    col_mean = jnp.sum(col_exp * logits, axis=0) / col_sum

    def exchange(axes, n, *stats):
        flat = jnp.concatenate(stats)
        size = flat.shape[0]
        pad = -size % 1024
        flat = jnp.pad(flat, (0, pad)).reshape(-1, 128)
        got = lax.all_to_all(jnp.broadcast_to(flat[None], (n,) + flat.shape), axes, 0, 0)
        return got.reshape(n, -1)

    got = exchange(CZ, NC * nz, row_top + jnp.log(row_sum), row_mean, row_part)
    row_lse, row_mean = merge(got[:, :rows], got[:, rows : 2 * rows])
    row_pos = jnp.sum(got[:, 2 * rows : 3 * rows], axis=0)
    row_total = 0.5 * jnp.sum(row_mean) - jnp.sum(row_pos)
    got = exchange(XY, peers, col_top + jnp.log(col_sum), col_mean, col_part, row_total[None])
    col_lse, col_mean = merge(got[:, :cols], got[:, cols : 2 * cols])
    col_pos = jnp.sum(got[:, 2 * cols : 3 * cols], axis=0)
    row_total = jnp.sum(got[:, 3 * cols])
    col_total = 0.5 * jnp.sum(col_mean)

    own = rows // NC
    row_loss = lax.dynamic_slice(row_lse - row_pos, (c * own,), (own,))
    col_loss = (col_lse - col_pos).reshape(peers, 1, part)
    other = lax.ppermute(col_loss, "c", SWAP)
    col_loss = jnp.where(
        c == 0, jnp.concatenate([col_loss, other], 1), jnp.concatenate([other, col_loss], 1)
    ).reshape(-1)

    grad_logits = 0.5 * (
        jnp.exp(logits - row_lse[:, None]) + jnp.exp(logits - col_lse[None, :])
    ) - hit.astype(jnp.float32)
    scaled_grad = (scale * grad_logits).astype(jnp.bfloat16)

    image_term = jnp.dot(scaled_grad, txt, preferred_element_type=jnp.float32)
    image_term = image_term.reshape(NC, nz, part, embed)
    keep = lax.dynamic_index_in_dim(image_term, c, 0, keepdims=False)
    send = lax.dynamic_index_in_dim(image_term, 1 - c, 0, keepdims=False).astype(jnp.bfloat16)
    both = keep + lax.ppermute(send, "c", SWAP).astype(jnp.float32)
    col_total = col_total + lax.ppermute(col_total[None], "c", SWAP)[0]
    extra = jnp.broadcast_to(col_total, (nz, 8, embed))
    both = jnp.concatenate([both, extra], axis=1)
    image_sum = lax.psum_scatter(both, "z", scatter_dimension=0, tiled=False)
    grad_image = image_sum[:part]

    text_term = lax.dot_general(
        scaled_grad, img, (((0,), (0,)), ((), ())), preferred_element_type=jnp.float32
    )
    text_term = text_term.astype(jnp.bfloat16).reshape(peers, part, embed)
    text_term = lax.all_to_all(text_term, XY, 0, 0)
    grad_text = jnp.sum(text_term.astype(jnp.float32), axis=0)

    temp_grad = (row_total + image_sum[part, 0]) / (rows * peers)
    return (row_loss, col_loss, grad_image, grad_text, temp_grad)


def solution(mesh):
    nz = mesh.shape["txt"]
    grid = Mesh(mesh.devices.reshape(NY, NX, NC, nz), ("y", "x", "c", "z"))
    images, texts = ("y", "x", "c", "z"), ("z", "y", "x", "c")
    in_specs = (P(images, None), P(texts, None), P(("y", "x", "c")), P())
    out_specs = (P(("y", "x", "c")), P("z"), P(images, None), P(texts, None), P())
    return jax.shard_map(local, mesh=grid, in_specs=in_specs, out_specs=out_specs, check_vma=False)
```

```python
import functools

import jax
import jax.numpy as jnp
from jax import lax
from jax.experimental import pallas as pl
from jax.experimental.pallas import tpu as pltpu
from jax.sharding import Mesh, PartitionSpec as P

NY, NX, NC = 4, 4, 2
XY = ("y", "x")
CZ = ("c", "z")
SWAP = [(0, 1), (1, 0)]
LANES = 128
F32 = jnp.float32
BF16 = jnp.bfloat16


def call(body, out_shape, *args, flops=0, smem=(), scratch=(), far=(), sent=()):
    places = {True: pl.BlockSpec(memory_space=pl.ANY), False: pl.BlockSpec(memory_space=pltpu.VMEM)}
    scalars = pl.BlockSpec(memory_space=pltpu.SMEM)
    many = isinstance(out_shape, tuple)
    outs = tuple(places[i in sent] for i in range(len(out_shape) if many else 1))
    size = sum(a.size * a.dtype.itemsize for a in args)
    return pl.pallas_call(
        body,
        out_shape=out_shape,
        in_specs=[scalars if i in smem else places[i in far] for i in range(len(args))],
        out_specs=outs if many else outs[0],
        scratch_shapes=scratch,
        cost_estimate=pl.CostEstimate(flops=flops, bytes_accessed=size, transcendentals=0),
        compiler_params=pltpu.CompilerParams(vmem_limit_bytes=16 * 1024 * 1024),
    )(*args)


def copies(sems, *pairs):
    started = [pltpu.make_async_copy(a, b, sems.at[i]) for i, (a, b) in enumerate(pairs)]
    for copy in started:
        copy.start()
    return started


def finish(started):
    for copy in started:
        copy.wait()


def dot(a, b, dims):
    return lax.dot_general(a, b, (dims, ((), ())), preferred_element_type=F32)


def spread_kernel(peers, txt, img, out, img_out, sems):
    finish(copies(sems, (img, img_out), *[(txt, out.at[p]) for p in range(peers)]))


def place_kernel(*refs):
    pieces, out, sems = refs[:-2], refs[-2], refs[-1]
    pairs, at = [], 0
    for piece in pieces:
        size = piece.shape[0]
        pairs.append((piece, out.at[at : at + size]))
        at += size
    finish(copies(sems, *pairs))


def pack(rows):
    tiles = []
    for row in rows:
        n = row.shape[1] // LANES
        tiles += [row[:, q * LANES : (q + 1) * LANES] for q in range(n)]
        tiles += [jnp.zeros((8 - n, LANES), F32)]
    return jnp.concatenate(tiles, axis=0)


def unpack(tile, n):
    return jnp.concatenate([tile[q : q + 1] for q in range(n)], axis=1)


def order_of(nz):
    first = [(who, k) for k in range(1, nz // 2) for who in (0, 1)] + [(0, nz // 2), (0, 0)]
    return first + [(1 - who, -k) for who, k in first]


def row_at(idx, block, nz, part):
    who, k = block
    c, z = idx[0], idx[1]
    core = c if who == 0 else 1 - c
    step = k * (1 - 2 * c)
    return pl.multiple_of((core * nz + lax.rem(z + step + nz, nz)) * part, 16)


def tall(rows):
    return jnp.concatenate(rows + [rows[-1]] * (8 - len(rows)), axis=0).T


def logits_kernel(peers, nz, idx, scale, own, oth, txt, pairs, logits, msg, txt_in, stat, column, packed, sems):
    half = own.shape[0]
    rows, cols = logits.shape
    part = rows // (NC * nz)
    loaded = copies(sems, *[(txt.at[n : n + 256], txt_in.at[n : n + 256]) for n in range(0, cols, 256)])
    column[...] = tall([unpack(pairs[...], rows // LANES)])
    s = scale[0]
    for i, n in enumerate(range(0, cols, 256)):
        loaded[i].wait()
        for at, images in ((0, own), (half, oth)):
            logits[at : at + half, n : n + 256] = s * dot(images[...], txt_in[n : n + 256, :], ((1,), (1,)))

    lane = lax.broadcasted_iota(jnp.int32, (part, LANES), 1)
    for i, block in enumerate(order_of(nz)):
        x = logits[i * part : (i + 1) * part, :]
        at = pl.ds(row_at(idx, block, nz, part), part)
        hit = lax.broadcasted_iota(jnp.int32, x.shape, 1) == column[at, 0:1].astype(jnp.int32)
        pos = jnp.sum(jnp.where(hit, x, 0.0), axis=1, keepdims=True)
        top = jnp.max(x, axis=1, keepdims=True)
        e = jnp.exp(x - top)
        total = jnp.sum(e, axis=1, keepdims=True)
        mean = jnp.sum(e * x, axis=1, keepdims=True) / total
        lse = top + jnp.log(total)
        stat[at, :] = jnp.where(lane == 0, lse, jnp.where(lane == 1, mean, jnp.where(lane == 2, pos, 0.0)))

    flat = stat[...].T
    packed[...] = pack([flat[0:1], flat[1:2], flat[2:3]])
    finish(copies(sems, *[(packed, msg.at[p]) for p in range(peers)]))


def columns_kernel(nz, idx, logits, pairs, out, column):
    rows, cols = logits.shape
    part = rows // (NC * nz)
    column[...] = tall([unpack(pairs[...], rows // LANES)])

    def fold(x):
        return x.reshape(part // 8, 8, cols)

    top = lax.fori_loop(
        0,
        rows // part,
        lambda i, m: jnp.maximum(m, jnp.max(fold(logits[pl.ds(pl.multiple_of(i * part, 16), part), :]), axis=0)),
        jnp.full((8, cols), -jnp.inf, F32),
    )
    top = jnp.max(top, axis=0, keepdims=True)
    total = moment = pos = jnp.zeros((8, cols), F32)
    for i, block in enumerate(order_of(nz)):
        x = logits[i * part : (i + 1) * part, :]
        at = pl.ds(row_at(idx, block, nz, part), part)
        hit = lax.broadcasted_iota(jnp.int32, x.shape, 1) == column[at, 0:1].astype(jnp.int32)
        e = jnp.exp(x - top)
        total += jnp.sum(fold(e), axis=0)
        moment += jnp.sum(fold(e * x), axis=0)
        pos += jnp.sum(fold(jnp.where(hit, x, 0.0)), axis=0)
    total = jnp.sum(total, axis=0, keepdims=True)
    moment = jnp.sum(moment, axis=0, keepdims=True)
    pos = jnp.sum(pos, axis=0, keepdims=True)
    out[...] = pack([top + jnp.log(total), moment / total, pos])


def merge(got):
    lse = got[:, 0:8, :]
    top = jnp.max(lse, axis=0)
    weight = jnp.exp(lse - top[None])
    total = jnp.sum(weight, axis=0)
    mean = jnp.sum(weight * got[:, 8:16, :], axis=0) / total
    return top + jnp.log(total), mean, jnp.sum(got[:, 16:24, :], axis=0)


def total_of(x):
    return jnp.sum(jnp.sum(x, axis=1, keepdims=True), axis=0, keepdims=True)


def rows_kernel(peers, count, got, stat, msg, lse_out, loss_out, packed, sems):
    lse, mean, pos = merge(got[...])
    row = lax.broadcasted_iota(jnp.int32, lse.shape, 0)
    used = row < count
    lse_out[...] = lse
    loss_out[...] = lse - pos
    total = total_of(jnp.where(used, 0.5 * mean - pos, 0.0))
    packed[...] = stat[...] + jnp.concatenate([jnp.where(row == count, total, 0.0), jnp.zeros((16, LANES), F32)], 0)
    finish(copies(sems, *[(packed, msg.at[p]) for p in range(peers)]))


def text_kernel(
    count, nz, idx, scale, got, logits, lse_in, pairs, own, oth, grad, text, loss_out, sums, column, blocks, sems
):
    half = own.shape[0]
    rows, cols = logits.shape
    part = rows // (NC * nz)
    s = scale[0]
    values = got[...]
    lse, mean, pos = merge(values)
    row = lax.broadcasted_iota(jnp.int32, lse.shape, 0)
    loss_out[...] = lse - pos
    col_total = total_of(jnp.where(row < count, 0.5 * mean, 0.0))
    row_total = total_of(jnp.where((row == count), jnp.sum(values[:, 0:8, :], axis=0), 0.0)) * (1.0 / LANES)
    sums[...] = jnp.where(row == 0, row_total, col_total)
    flat = unpack(lse, count)
    column[...] = tall([unpack(lse_in[...], count), unpack(pairs[...], count)])

    for i, block in enumerate(order_of(nz)):
        x = logits[i * part : (i + 1) * part, :]
        at = pl.ds(row_at(idx, block, nz, part), part)
        hit = lax.broadcasted_iota(jnp.int32, x.shape, 1) == column[at, 1:2].astype(jnp.int32)
        value = 0.5 * (jnp.exp(x - column[at, 0:1]) + jnp.exp(x - flat)) - jnp.where(hit, 1.0, 0.0)
        grad[i * part : (i + 1) * part, :] = (s * value).astype(BF16)

    started = []
    for i, n in enumerate(range(0, own.shape[1], 256)):
        block = dot(grad[:half, :], own[:, n : n + 256], ((0,), (0,)))
        block += dot(grad[half:, :], oth[:, n : n + 256], ((0,), (0,)))
        blocks[:, n : n + 256] = block.astype(BF16)
        started.append(pltpu.make_async_copy(blocks.at[:, n : n + 256], text.at[:, n : n + 256], sems.at[i]))
        started[-1].start()
    finish(started)


def image_kernel(grad, txt, keep, send, txt_in, sems):
    half, embed = keep.shape
    cuts = range(0, embed, 256)
    loaded = copies(sems, *[(txt.at[:, n : n + 256], txt_in.at[:, n : n + 256]) for n in cuts])
    for i, n in enumerate(cuts):
        loaded[i].wait()
        cut = txt_in[:, n : n + 256]
        send[:, n : n + 256] = dot(grad[half:, :], cut, ((1,), (0,))).astype(BF16)
        keep[:, n : n + 256] = dot(grad[:half, :], cut, ((1,), (0,)))


def pieces_kernel(keep, received, sums, other_sums, own, *outs):
    part, embed = own.shape
    total = sums[1:2, :] + other_sums[1:2, :]
    high = total.astype(BF16)
    rest = total - high.astype(F32)
    middle = rest.astype(BF16)
    low = (rest - middle.astype(F32)).astype(BF16)
    at = 0
    for out in outs:
        size = out.shape[0]
        out[:, :embed] = (keep[at : at + size, :] + received[at : at + size, :].astype(F32)).astype(BF16)
        lane = lax.broadcasted_iota(jnp.int32, (size, LANES), 1)
        tail = jnp.where(lane == 0, high.astype(F32), jnp.where(lane == 1, middle.astype(F32), low.astype(F32)))
        out[:, embed:] = tail.astype(BF16)
        at += size
    own[...] = keep[at:, :] + received[at:, :].astype(F32)


def tail_of(ref, embed):
    tail = ref[0:16, embed:].astype(F32)[0:8]
    lane = lax.broadcasted_iota(jnp.int32, tail.shape, 1)
    return jnp.sum(jnp.where(lane < 3, tail, 0.0), axis=1, keepdims=True)


def chip_sum_kernel(sums, other_sums, own, *refs):
    arrived, keep, send = refs[:-2], refs[-2], refs[-1]
    part, embed = own.shape
    mine = own[...]
    theirs = jnp.zeros(own.shape, F32)
    tail = jnp.zeros((8, 1), F32)
    for ref in arrived:
        mine = mine + ref[0:part, :embed].astype(F32)
        if ref.shape[0] > part:
            theirs = theirs + ref[part:, :embed].astype(F32)
            tail = tail + tail_of(ref, embed)
    keep[:, :embed] = mine
    send[:, :embed] = theirs
    send[:, embed:] = jnp.zeros((part, LANES), F32)
    send[0:8, embed:] = jnp.broadcast_to(tail, (8, LANES))
    both = tail_of(arrived[-1], embed) + sums[1:2, :] + other_sums[1:2, :]
    keep[:, embed:] = jnp.zeros((part, LANES), F32)
    keep[0:8, embed:] = tail + both + sums[0:1, :]


def image_sum_kernel(scale, keep, received, out, temp):
    embed = out.shape[1]
    out[...] = keep[:, :embed] + received[:, :embed]
    temp[...] = (keep[0:8, embed:] + received[0:8, embed:]) * scale[0]


def text_sum_kernel(got, out):
    out[...] = jnp.sum(got[...].astype(F32), axis=0)


def local(image_embed, text_embed, pair_col, log_scale):
    part, embed = image_embed.shape
    peers = NY * NX
    nz = lax.axis_size("z")
    half = nz * part
    rows, cols = NC * half, peers * part
    count = rows // LANES
    batch = peers * rows
    c = lax.axis_index("c")
    z = lax.axis_index("z")
    idx = jnp.stack([c, z])
    scale = jnp.exp(log_scale)
    scale1 = scale[None]
    sds = jax.ShapeDtypeStruct
    sems = lambda n: pltpu.SemaphoreType.DMA((n,))
    last = nz // 2

    def swap(x):
        return lax.ppermute(x, "c", SWAP)

    def ahead(x, k):
        pairs = [((i + k) % nz, i) for i in range(nz)]
        return lax.ppermute(x, CZ, pairs + [(nz + i, nz + (i + k) % nz) for i in range(nz)])

    def onward(x, k):
        pairs = [(i, (i + k) % nz) for i in range(nz)]
        return lax.ppermute(x, CZ, pairs + [(nz + (i + k) % nz, nz + i) for i in range(nz)])

    spread, image = call(
        functools.partial(spread_kernel, peers),
        (sds((peers, part, embed), BF16), sds((part, embed), BF16)),
        text_embed,
        image_embed,
        far=(0, 1),
        sent=(0, 1),
        scratch=[sems(peers + 1)],
    )
    txt = lax.all_to_all(spread, XY, 0, 0).reshape(cols, embed)
    chip = jnp.concatenate([image, swap(image)])
    got = [ahead(image, last)] + [ahead(chip, k) for k in range(last - 1, 0, -1)]
    own = call(
        place_kernel,
        sds((half, embed), BF16),
        *got[:0:-1],
        got[0],
        image,
        far=range(last + 1),
        scratch=[sems(last + 1)],
    )
    oth = swap(own)

    rem = pair_col % (cols * NC)
    block = rem // part
    ours = pair_col // (cols * NC) == z
    place = (block // NC * part + rem % part).astype(F32)
    mine = jnp.where(ours & (block % NC == c), place, -1.0)
    theirs = swap(jnp.where(ours & (block % NC == 1 - c), place, -1.0))
    pairs = jnp.where(c == 0, jnp.concatenate([mine, theirs]), jnp.concatenate([theirs, mine]))
    pairs = jnp.pad(pairs, (0, 8 * LANES - rows)).reshape(8, LANES)

    work = 2 * rows * cols * embed
    logits, msg = call(
        functools.partial(logits_kernel, NC * nz, nz),
        (sds((rows, cols), F32), sds((NC * nz, 24, LANES), F32)),
        idx,
        scale1,
        own,
        oth,
        txt,
        pairs,
        flops=work,
        smem=(0, 1),
        far=(4,),
        sent=(1,),
        scratch=[
            pltpu.VMEM((cols, embed), BF16),
            pltpu.VMEM((rows, LANES), F32),
            pltpu.VMEM((rows, 8), F32),
            pltpu.VMEM((24, LANES), F32),
            sems(NC * nz),
        ],
    )
    row_got = lax.all_to_all(msg, CZ, 0, 0)
    stat = call(
        functools.partial(columns_kernel, nz),
        sds((24, LANES), F32),
        idx,
        logits,
        pairs,
        flops=8 * rows * cols,
        smem=(0,),
        scratch=[pltpu.VMEM((rows, 8), F32)],
    )
    msg, row_lse, row_loss = call(
        functools.partial(rows_kernel, peers, count),
        (sds((peers, 24, LANES), F32), sds((8, LANES), F32), sds((8, LANES), F32)),
        row_got,
        stat,
        sent=(0,),
        scratch=[pltpu.VMEM((24, LANES), F32), sems(peers)],
    )
    col_got = lax.all_to_all(msg, XY, 0, 0)
    row_loss = lax.dynamic_slice(row_loss, (c * (count // NC), 0), (count // NC, LANES)).reshape(-1)

    grad, text_term, col_loss, sums = call(
        functools.partial(text_kernel, count, nz),
        (sds((rows, cols), BF16), sds((cols, embed), BF16), sds((8, LANES), F32), sds((8, LANES), F32)),
        idx,
        scale1,
        col_got,
        logits,
        row_lse,
        pairs,
        own,
        oth,
        flops=work,
        smem=(0, 1),
        sent=(1,),
        scratch=[pltpu.VMEM((rows, 8), F32), pltpu.VMEM((cols, embed), BF16), sems(embed // 256)],
    )
    text_got = lax.all_to_all(text_term.reshape(peers, part, embed), XY, 0, 0)
    keep, send = call(
        image_kernel,
        (sds((half, embed), F32), sds((half, embed), BF16)),
        grad,
        txt,
        flops=work,
        far=(1,),
        scratch=[pltpu.VMEM((cols, embed), BF16), sems(embed // 256)],
    )
    received = swap(send)
    other_sums = swap(sums)
    shapes = [sds((NC * part, embed + LANES), BF16)] * (last - 1) + [sds((part, embed + LANES), BF16)]
    own_sum, *outs = call(
        pieces_kernel, (sds((part, embed), F32), *shapes), keep, received, sums, other_sums
    )
    arrived = {k: onward(outs[k - 1], k) for k in range(last, 0, -1)}
    wide = sds((part, embed + LANES), F32)
    keep, send = call(
        chip_sum_kernel, (wide, wide), sums, other_sums, own_sum, *[arrived[k] for k in range(1, last + 1)]
    )
    grad_image, temp = call(
        image_sum_kernel,
        (sds((part, embed), F32), sds((8, LANES), F32)),
        jnp.full((1,), 1.0 / batch, F32),
        keep,
        swap(send),
        smem=(0,),
    )

    col_loss = col_loss[:count].reshape(peers, 1, part)
    other = swap(col_loss)
    col_loss = jnp.where(
        c == 0, jnp.concatenate([col_loss, other], 1), jnp.concatenate([other, col_loss], 1)
    ).reshape(-1)
    grad_text = call(text_sum_kernel, sds((part, embed), F32), text_got)
    return (row_loss, col_loss, grad_image, grad_text, temp[0, 0])


def solution(mesh):
    nz = mesh.shape["txt"]
    grid = Mesh(mesh.devices.reshape(NY, NX, NC, nz), ("y", "x", "c", "z"))
    images, texts = ("y", "x", "c", "z"), ("z", "y", "x", "c")
    in_specs = (P(images, None), P(texts, None), P(("y", "x", "c")), P())
    out_specs = (P(("y", "x", "c")), P("z"), P(images, None), P(texts, None), P())
    return jax.shard_map(local, mesh=grid, in_specs=in_specs, out_specs=out_specs, check_vma=False)
```

```python
import functools

import jax
import jax.numpy as jnp
from jax import lax
from jax.experimental import pallas as pl
from jax.experimental.pallas import tpu as pltpu
from jax.sharding import Mesh, PartitionSpec as P

NY, NX, NC = 4, 4, 2
XY = ("y", "x")
CZ = ("c", "z")
SWAP = [(0, 1), (1, 0)]
LANES = 128
VMEM_BYTES = 64 * 1024 * 1024
F32 = jnp.float32
BF16 = jnp.bfloat16


class Loaded:
    def __init__(self, source, ref, sems, cut):
        self.ref = ref
        self.started = []
        axis, size = cut
        for i, at in enumerate(range(0, ref.shape[axis], size)):
            window = (slice(None),) * axis + (slice(at, at + size),)
            self.started.append(pltpu.make_async_copy(source.at[window], ref.at[window], sems.at[i]))

    def start(self):
        for copy in self.started:
            copy.start()

    def part(self, i):
        self.started[i].wait()

    def get(self):
        for i in range(len(self.started)):
            self.part(i)
        return self.ref


class Joined(Loaded):
    def __init__(self, sources, ref, sems):
        self.ref = ref
        self.started = []
        at = 0
        for i, source in enumerate(sources):
            size = source.shape[0]
            self.started.append(pltpu.make_async_copy(source, ref.at[at : at + size], sems.at[i]))
            at += size


class Sender:
    def __init__(self, sems):
        self.sems = sems
        self.started = []

    def send(self, source, target):
        copy = pltpu.make_async_copy(source, target, self.sems.at[len(self.started)])
        copy.start()
        self.started.append(copy)

    def finish(self):
        for copy in self.started:
            copy.wait()


def call(body, out_shape, *args, flops=0, smem=(), scratch=(), cuts=(), joined=None, held=None, sends=16):
    many = isinstance(out_shape, tuple)
    shapes = out_shape if many else (out_shape,)
    held = [x if held is None or held[i] is None else held[i] for i, x in enumerate(shapes)]
    cuts = dict(cuts)
    joined = len(args) if joined is None else joined
    arrays = [i for i in range(joined) if i not in smem]
    plan = [cuts.get(i, (0, args[i].shape[0])) for i in arrays]
    counts = [-(-args[i].shape[axis] // size) for i, (axis, size) in zip(arrays, plan)]
    buffers_of = [pltpu.VMEM(args[i].shape, args[i].dtype) for i in arrays]
    if joined < len(args):
        counts.append(len(args) - joined)
        last = args[-1]
        buffers_of.append(pltpu.VMEM((sum(a.shape[0] for a in args[joined:]), last.shape[1]), last.dtype))

    def kernel(*refs):
        ins, refs = refs[: len(args)], refs[len(args) :]
        outs, refs = refs[: len(shapes)], refs[len(shapes) :]
        buffers, refs = refs[: len(buffers_of)], refs[len(buffers_of) :]
        spare, refs = refs[: len(held)], refs[len(held) :]
        in_sems, refs = refs[: len(counts)], refs[len(counts) :]
        out_sems, refs = refs[0], refs[1:]
        given = list(ins[:joined])
        for j, i in enumerate(arrays):
            given[i] = Loaded(ins[i], buffers[j], in_sems[j], plan[j])
            given[i].start()
        if joined < len(args):
            given.append(Joined(ins[joined:], buffers[-1], in_sems[-1]))
            given[-1].start()
        sender = Sender(out_sems)
        body(given, spare, outs, sender, *refs)
        sender.finish()

    far = pl.BlockSpec(memory_space=pltpu.HBM)
    scalars = pl.BlockSpec(memory_space=pltpu.SMEM)
    size = sum(a.size * a.dtype.itemsize for a in args)
    return pl.pallas_call(
        kernel,
        out_shape=out_shape,
        in_specs=[scalars if i in smem else far for i in range(len(args))],
        out_specs=tuple(far for _ in shapes) if many else far,
        scratch_shapes=[
            *buffers_of,
            *[pltpu.VMEM(x.shape, x.dtype) for x in held],
            *[pltpu.SemaphoreType.DMA((n,)) for n in counts],
            pltpu.SemaphoreType.DMA((sends,)),
            *scratch,
        ],
        cost_estimate=pl.CostEstimate(flops=flops, bytes_accessed=size, transcendentals=0),
        compiler_params=pltpu.CompilerParams(vmem_limit_bytes=VMEM_BYTES),
    )(*args)


def near(body, out_shape, *args, smem=(), unread=()):
    spec = lambda i: pl.BlockSpec(memory_space=pltpu.SMEM if i in smem else pltpu.HBM if i in unread else pltpu.VMEM)
    many = isinstance(out_shape, tuple)
    vmem = pl.BlockSpec(memory_space=pltpu.VMEM)
    return pl.pallas_call(
        body,
        out_shape=out_shape,
        in_specs=[spec(i) for i in range(len(args))],
        out_specs=tuple(vmem for _ in out_shape) if many else vmem,
        compiler_params=pltpu.CompilerParams(vmem_limit_bytes=8 * 1024 * 1024),
    )(*args)


def dot(a, b, dims):
    return lax.dot_general(a, b, (dims, ((), ())), preferred_element_type=F32)


def pack(rows):
    tiles = []
    for row in rows:
        n = row.shape[1] // LANES
        tiles += [row[:, q * LANES : (q + 1) * LANES] for q in range(n)]
        tiles += [jnp.zeros((8 - n, LANES), F32)]
    return jnp.concatenate(tiles, axis=0)


def unpack(tile, n):
    return jnp.concatenate([tile[q : q + 1] for q in range(n)], axis=1)


def order_of(nz):
    first = [(who, k) for k in range(1, nz // 2) for who in (0, 1)] + [(0, nz // 2), (0, 0)]
    return first + [(1 - who, -k) for who, k in first]


def row_at(idx, block, nz, part):
    who, k = block
    c, z = idx[0], idx[1]
    core = c if who == 0 else 1 - c
    step = k * (1 - 2 * c)
    return pl.multiple_of((core * nz + lax.rem(z + step + nz, nz)) * part, 16)


def tall(rows):
    return jnp.concatenate(rows + [rows[-1]] * (8 - len(rows)), axis=0).T


def logits_kernel(nz, ins, held, outs, sender, column, stat):
    idx, scale, pairs, txt, images = ins
    logits, row_out, packed = held
    rows, cols = logits.shape
    part = rows // (NC * nz)
    s = scale[0]
    column[...] = tall([unpack(pairs.get(), rows // LANES)])
    images = images.get()
    for i, n in enumerate(range(0, cols, 256)):
        txt.part(i)
        for m in range(0, rows, 384):
            block = dot(images[m : m + 384, :], txt.ref[n : n + 256, :], ((1,), (1,)))
            logits[m : m + 384, n : n + 256] = s * block
    sender.send(logits, outs[0])

    def fold(x):
        return x.reshape(part // 8, 8, cols)

    col_top = jnp.full((8, cols), -jnp.inf, F32)
    col_pos = jnp.zeros((8, cols), F32)
    lane = lax.broadcasted_iota(jnp.int32, (part, LANES), 1)
    for i, block in enumerate(order_of(nz)):
        x = logits[i * part : (i + 1) * part, :]
        col_top = jnp.maximum(col_top, jnp.max(fold(x), axis=0))
        at = pl.ds(row_at(idx, block, nz, part), part)
        hit = lax.broadcasted_iota(jnp.int32, x.shape, 1) == column[at, 0:1].astype(jnp.int32)
        paired = jnp.where(hit, x, 0.0)
        col_pos += jnp.sum(fold(paired), axis=0)
        pos = jnp.sum(paired, axis=1, keepdims=True)
        top = jnp.max(x, axis=1, keepdims=True)
        e = jnp.exp(x - top)
        total = jnp.sum(e, axis=1, keepdims=True)
        mean = jnp.sum(e * x, axis=1, keepdims=True) / total
        lse = top + jnp.log(total)
        stat[at, :] = jnp.where(lane == 0, lse, jnp.where(lane == 1, mean, jnp.where(lane == 2, pos, 0.0)))
    flat = stat[...].T
    row_out[...] = pack([flat[0:1], flat[1:2], flat[2:3]])
    sender.send(row_out, outs[1])

    top = jnp.max(col_top, axis=0, keepdims=True)
    total = moment = jnp.zeros((8, cols), F32)
    for i in range(NC * nz):
        x = logits[i * part : (i + 1) * part, :]
        e = jnp.exp(x - top)
        total += jnp.sum(fold(e), axis=0)
        moment += jnp.sum(fold(e * x), axis=0)
    total = jnp.sum(total, axis=0, keepdims=True)
    moment = jnp.sum(moment, axis=0, keepdims=True)
    pos = jnp.sum(col_pos, axis=0, keepdims=True)
    packed[...] = pack([top + jnp.log(total), moment / total, pos])
    for p in range(outs[2].shape[0]):
        sender.send(packed, outs[2].at[p])


def merge(got):
    lse = [x[0:8, :] for x in got]
    top = functools.reduce(jnp.maximum, lse)
    weight = [jnp.exp(x - top) for x in lse]
    total = sum(weight)
    mean = sum(w * x[8:16, :] for w, x in zip(weight, got)) / total
    return top + jnp.log(total), mean, sum(x[16:24, :] for x in got)


def total_of(x):
    return jnp.sum(jnp.sum(x, axis=1, keepdims=True), axis=0, keepdims=True)


def split_tail(total, size):
    high = total.astype(BF16)
    rest = total - high.astype(F32)
    middle = rest.astype(BF16)
    low = (rest - middle.astype(F32)).astype(BF16)
    lane = lax.broadcasted_iota(jnp.int32, (size, LANES), 1)
    tail = jnp.where(lane == 0, high.astype(F32), jnp.where(lane == 1, middle.astype(F32), low.astype(F32)))
    return tail.astype(BF16)


def tail_of(ref, embed):
    tail = ref[0:16, embed:].astype(F32)[0:8]
    lane = lax.broadcasted_iota(jnp.int32, tail.shape, 1)
    return jnp.sum(jnp.where(lane < 3, tail, 0.0), axis=1, keepdims=True)


def grad_kernel(count, nz, ins, held, outs, sender, column, grad, turned):
    idx, scale, col_got, chip, across, mine, theirs, pairs, logits, txt, images = ins
    text, send, first, row_loss, col_loss, sums = held
    half, embed = send.shape
    rows, cols = grad.shape
    part = rows // (NC * nz)
    s = scale[0]
    used = lax.broadcasted_iota(jnp.int32, (8, LANES), 0) < count
    row_lse, row_mean, row_pos = merge([r.get()[...] for r in (chip, across, mine, theirs)])
    row_loss[...] = row_lse - row_pos
    sender.send(row_loss, outs[3])
    row_total = total_of(jnp.where(used, 0.5 * row_mean - row_pos, 0.0))
    col_ref = col_got.get()
    col_lse, col_mean, col_pos = merge([col_ref[p] for p in range(col_ref.shape[0])])
    col_loss[...] = col_lse - col_pos
    sender.send(col_loss, outs[4])
    col_total = total_of(jnp.where(used, 0.5 * col_mean, 0.0))
    sums[...] = jnp.broadcast_to(col_total, sums.shape)
    sender.send(sums, outs[5])
    text[:, embed:] = split_tail(jnp.broadcast_to(row_total, (1, LANES)), cols)
    sender.send(text.at[:, embed:], outs[0].at[:, embed:])
    flat = unpack(col_lse, count)
    column[...] = tall([unpack(row_lse, count), unpack(pairs.get(), count)])

    for i, block in enumerate(order_of(nz)):
        logits.part(i)
        x = logits.ref[i * part : (i + 1) * part, :]
        at = pl.ds(row_at(idx, block, nz, part), part)
        hit = lax.broadcasted_iota(jnp.int32, x.shape, 1) == column[at, 1:2].astype(jnp.int32)
        value = 0.5 * (jnp.exp(x - column[at, 0:1]) + jnp.exp(x - flat)) - jnp.where(hit, 1.0, 0.0)
        grad[i * part : (i + 1) * part, :] = (s * value).astype(BF16)
    first[...] = grad[:half, :]
    sender.send(first, outs[2])

    cuts = range(0, embed, 256)
    for i, n in enumerate(cuts):
        txt.part(i)
        send[:, n : n + 256] = dot(grad[half:, :], txt.ref[:, n : n + 256], ((1,), (0,))).astype(BF16)
        sender.send(send.at[:, n : n + 256], outs[1].at[:, n : n + 256])
    turned[...] = grad[...].T
    images = images.get()
    for n in cuts:
        text[:, n : n + 256] = dot(turned[...], images[:, n : n + 256], ((1,), (0,))).astype(BF16)
        sender.send(text.at[:, n : n + 256], outs[0].at[:, n : n + 256])


def image_kernel(ins, held, outs, sender):
    sums, other_sums, first, txt, received = ins
    total = sums.get()[0:1, :] + other_sums.get()[0:1, :]
    grad = first.get()
    embed = received.ref.shape[1]
    for i, n in enumerate(range(0, embed, 256)):
        txt.part(i)
        received.part(i)
        block = dot(grad[...], txt.ref[:, n : n + 256], ((1,), (0,)))
        block += received.ref[:, n : n + 256].astype(F32)
        at = 0
        for ref in held:
            size = ref.shape[0]
            ref[:, n : n + 256] = block[at : at + size].astype(ref.dtype)
            at += size
    for ref, out in zip(held, outs):
        if ref.shape[1] > embed:
            ref[:, embed:] = split_tail(total, ref.shape[0])
        sender.send(ref, out)


def forward_kernel(idx, sums, other_sums, own, near_one, far_one, out):
    part, embed = own.shape[0] // NC, own.shape[1]
    total = own[...] + near_one[:, :embed].astype(F32)
    out[:part, :embed] = (total[:part] + far_one[:, :embed].astype(F32)).astype(BF16)
    out[part:, :embed] = total[part:].astype(BF16)
    across = jnp.where(idx[0] == 0, 1.0, 0.0) * tail_of(far_one, embed)
    tail = sums[0:1, :] + other_sums[0:1, :] + tail_of(near_one, embed)[0:1] + across[0:1]
    out[:, embed:] = split_tail(tail, NC * part)


def chip_sum_kernel(sums, other_sums, own, one, two, row_total, *refs):
    keep, send = refs[-2], refs[-1]
    part, embed = own.shape
    total = one[:, :embed].astype(F32) + two[:, :embed].astype(F32)
    tail = tail_of(one, embed) + tail_of(two, embed)
    send[:, :embed] = total[part:]
    send[:, embed:] = jnp.zeros((part, LANES), F32)
    send[0:8, embed:] = jnp.broadcast_to(tail, (8, LANES))
    keep[:, :embed] = own[...] + total[:part]
    keep[:, embed:] = jnp.zeros((part, LANES), F32)
    keep[0:8, embed:] = tail + sums[...] + other_sums[...] + row_total[...]


def text_sum_kernel(got, out, total):
    embed = out.shape[1]
    out[...] = jnp.sum(got[:, :, :embed].astype(F32), axis=0)
    tail = sum(tail_of(got.at[p], embed) for p in range(got.shape[0]))
    total[...] = jnp.broadcast_to(tail, total.shape)


def image_sum_kernel(scale, keep, received, out, temp):
    embed = out.shape[1]
    out[...] = keep[:, :embed] + received[:, :embed]
    temp[...] = (keep[0:1, embed : embed + 1] + received[0:1, embed : embed + 1]) * scale[0]


def local(image_embed, text_embed, pair_col, log_scale):
    part, embed = image_embed.shape
    peers = NY * NX
    nz = lax.axis_size("z")
    half = nz * part
    rows, cols = NC * half, peers * part
    count = rows // LANES
    batch = peers * rows
    c = lax.axis_index("c")
    z = lax.axis_index("z")
    idx = jnp.stack([c, z])
    scale = jnp.exp(log_scale)
    scale1 = scale[None]
    sds = jax.ShapeDtypeStruct
    vmem = pltpu.VMEM
    last = nz // 2

    def swap(x):
        return lax.ppermute(x, "c", SWAP)

    def ahead(x, k):
        pairs = [((i + k) % nz, i) for i in range(nz)]
        return lax.ppermute(x, CZ, pairs + [(nz + i, nz + (i + k) % nz) for i in range(nz)])

    def onward(x, k):
        pairs = [(i, (i + k) % nz) for i in range(nz)]
        return lax.ppermute(x, CZ, pairs + [(nz + (i + k) % nz, nz + i) for i in range(nz)])

    spread = jnp.broadcast_to(text_embed[None], (peers, part, embed))
    txt = lax.all_to_all(spread, XY, 0, 0).reshape(cols, embed)
    partner = swap(image_embed)
    chip = jnp.concatenate([image_embed, partner])
    got = [ahead(chip, 1), ahead(chip, 2)]
    got += [ahead(got[1], 1), ahead(got[1][:part], 2)]
    images = got + [image_embed] + [swap(x) for x in got] + [partner]

    rem = pair_col % (cols * NC)
    block = rem // part
    ours = pair_col // (cols * NC) == z
    place = (block // NC * part + rem % part).astype(F32)
    mine = jnp.where(ours & (block % NC == c), place, -1.0)
    theirs = swap(jnp.where(ours & (block % NC == 1 - c), place, -1.0))
    pairs = jnp.where(c == 0, jnp.concatenate([mine, theirs]), jnp.concatenate([theirs, mine]))
    pairs = jnp.pad(pairs, (0, 8 * LANES - rows)).reshape(8, LANES)

    work = 2 * rows * cols * embed
    tile, pad = sds((24, LANES), F32), sds((8, LANES), F32)
    logits, stat, msg = call(
        functools.partial(logits_kernel, nz),
        (sds((rows, cols), F32), tile, sds((peers, 24, LANES), F32)),
        idx,
        scale1,
        pairs,
        txt,
        *images,
        flops=work,
        smem=(0, 1),
        cuts={3: (0, 256)},
        joined=4,
        held=(None, None, tile),
        sends=2 + peers,
        scratch=[vmem((rows, 8), F32), vmem((rows, LANES), F32)],
    )
    col_got = lax.all_to_all(msg, XY, 0, 0)
    chip_stat = jnp.concatenate(merge([stat, swap(stat)]))
    stats = [ahead(chip_stat, k) for k in range(last, 0, -1)]
    merged = jnp.concatenate(merge(stats[1:]))

    wide = embed + LANES
    text_term, send, first, row_loss, col_loss, sums = call(
        functools.partial(grad_kernel, count, nz),
        (sds((cols, wide), BF16), sds((half, embed), BF16), sds((half, cols), BF16), pad, pad, pad),
        idx,
        scale1,
        col_got,
        chip_stat,
        stats[0],
        merged,
        swap(merged),
        pairs,
        logits,
        txt,
        *images,
        flops=2 * work,
        smem=(0, 1),
        cuts={8: (0, part), 9: (1, 256)},
        joined=10,
        sends=5 + 2 * (embed // 256),
        scratch=[vmem((rows, 8), F32), vmem((rows, cols), BF16), vmem((cols, rows), BF16)],
    )
    received = swap(send)
    other_sums = swap(sums)
    text_got = lax.all_to_all(text_term.reshape(peers, part, wide), XY, 0, 0)
    one, two, three, four, own = call(
        image_kernel,
        (
            sds((NC * part, wide), BF16),
            sds((NC * part, embed), F32),
            sds((NC * part, wide), BF16),
            sds((part, wide), BF16),
            sds((part, embed), F32),
        ),
        sums,
        other_sums,
        first,
        txt,
        received,
        flops=work // 2,
        cuts={3: (1, 256), 4: (1, 256)},
    )
    two = near(
        forward_kernel,
        sds((NC * part, wide), BF16),
        idx,
        sums,
        other_sums,
        two,
        onward(three, 1),
        onward(four, 2),
        smem=(0,),
    )
    row_loss = lax.dynamic_slice(row_loss, (c * (count // NC), 0), (count // NC, LANES)).reshape(-1)
    col_loss = col_loss[:count].reshape(peers, 1, part)
    other = swap(col_loss)
    col_loss = jnp.where(
        c == 0, jnp.concatenate([col_loss, other], 1), jnp.concatenate([other, col_loss], 1)
    ).reshape(-1)
    grad_text, row_total = near(text_sum_kernel, (sds((part, embed), F32), pad), text_got)
    keep, send = near(
        chip_sum_kernel,
        (sds((part, wide), F32), sds((part, wide), F32)),
        sums,
        other_sums,
        own,
        onward(one, 1),
        onward(two, 2),
        row_total,
        row_loss,
        col_loss,
        unread=(6, 7),
    )
    grad_image, temp = near(
        image_sum_kernel,
        (sds((part, embed), F32), sds((1, 1), F32)),
        jnp.full((1,), 1.0 / batch, F32),
        keep,
        swap(send),
        smem=(0,),
    )
    return (row_loss, col_loss, grad_image, grad_text, temp[0, 0])


def solution(mesh):
    nz = mesh.shape["txt"]
    grid = Mesh(mesh.devices.reshape(NY, NX, NC, nz), ("y", "x", "c", "z"))
    images, texts = ("y", "x", "c", "z"), ("z", "y", "x", "c")
    in_specs = (P(images, None), P(texts, None), P(("y", "x", "c")), P())
    out_specs = (P(("y", "x", "c")), P("z"), P(images, None), P(texts, None), P())
    return jax.shard_map(local, mesh=grid, in_specs=in_specs, out_specs=out_specs, check_vma=False)
```

```python
import functools

import jax
import jax.numpy as jnp
from jax import lax
from jax.experimental import pallas as pl
from jax.experimental.pallas import tpu as pltpu
from jax.sharding import Mesh, PartitionSpec as P

NY, NX, NC = 4, 4, 2
XY = ("y", "x")
CZ = ("c", "z")
SWAP = [(0, 1), (1, 0)]
LANES = 128
VMEM_BYTES = 64 * 1024 * 1024
MESSAGE = 48
F32 = jnp.float32
BF16 = jnp.bfloat16


class Loaded:
    def __init__(self, source, ref, sems, cut):
        self.ref = ref
        self.started = []
        axis, size = cut
        for i, at in enumerate(range(0, ref.shape[axis], size)):
            window = (slice(None),) * axis + (slice(at, at + size),)
            self.started.append(pltpu.make_async_copy(source.at[window], ref.at[window], sems.at[i]))

    def start(self):
        for copy in self.started:
            copy.start()

    def start_part(self, i):
        self.started[i].start()

    def part(self, i):
        self.started[i].wait()

    def get(self):
        for i in range(len(self.started)):
            self.part(i)
        return self.ref


class Joined(Loaded):
    def __init__(self, sources, ref, sems):
        self.ref = ref
        self.started = []
        at = 0
        for i, source in enumerate(sources):
            size = source.shape[0]
            self.started.append(pltpu.make_async_copy(source, ref.at[at : at + size], sems.at[i]))
            at += size


class Sender:
    def __init__(self, sems):
        self.sems = sems
        self.started = []

    def send(self, source, target):
        copy = pltpu.make_async_copy(source, target, self.sems.at[len(self.started)])
        copy.start()
        self.started.append(copy)

    def finish(self):
        for copy in self.started:
            copy.wait()


def call(body, out_shape, *args, flops=0, smem=(), scratch=(), cuts=(), joined=None, held=None, sends=16, spare=0, later=()):
    many = isinstance(out_shape, tuple)
    shapes = out_shape if many else (out_shape,)
    held = [x if held is None or held[i] is None else held[i] for i, x in enumerate(shapes)]
    cuts = dict(cuts)
    joined = len(args) if joined is None else joined
    arrays = [i for i in range(joined) if i not in smem]
    plan = [cuts.get(i, (0, args[i].shape[0])) for i in arrays]
    counts = [-(-args[i].shape[axis] // size) for i, (axis, size) in zip(arrays, plan)]
    buffers_of = [pltpu.VMEM(args[i].shape, args[i].dtype) for i in arrays]
    if joined < len(args):
        counts.append(len(args) - joined)
        last = args[-1]
        buffers_of.append(pltpu.VMEM((sum(a.shape[0] for a in args[joined:]), last.shape[1]), last.dtype))

    def kernel(*refs):
        ins, refs = refs[: len(args)], refs[len(args) :]
        outs, refs = refs[: len(shapes)], refs[len(shapes) :]
        buffers, refs = refs[: len(buffers_of)], refs[len(buffers_of) :]
        kept, refs = refs[: len(held)], refs[len(held) :]
        in_sems, refs = refs[: len(counts)], refs[len(counts) :]
        out_sems, refs = refs[0], refs[1:]
        given = list(ins[:joined])
        for j, i in enumerate(arrays):
            given[i] = Loaded(ins[i], buffers[j], in_sems[j], plan[j])
            if i not in later:
                given[i].start()
        if joined < len(args):
            given.append(Joined(ins[joined:], buffers[-1], in_sems[-1]))
            if joined not in later:
                given[-1].start()
        sender = Sender(out_sems)
        body(given, kept, outs, sender, *refs)
        sender.finish()

    far = pl.BlockSpec(memory_space=pl.ANY if spare else pltpu.HBM)
    scalars = pl.BlockSpec(memory_space=pltpu.SMEM)
    size = sum(a.size * a.dtype.itemsize for a in args)
    return pl.pallas_call(
        kernel,
        out_shape=out_shape,
        in_specs=[scalars if i in smem else far for i in range(len(args))],
        out_specs=tuple(far for _ in shapes) if many else far,
        scratch_shapes=[
            *buffers_of,
            *[pltpu.VMEM(x.shape, x.dtype) for x in held],
            *[pltpu.SemaphoreType.DMA((n,)) for n in counts],
            pltpu.SemaphoreType.DMA((sends,)),
            *scratch,
        ],
        cost_estimate=pl.CostEstimate(flops=flops, bytes_accessed=size, transcendentals=0),
        compiler_params=pltpu.CompilerParams(vmem_limit_bytes=VMEM_BYTES - spare),
    )(*args)


def small(body, out_shape, *args, smem=(), unread=()):
    spec = lambda i: pl.BlockSpec(memory_space=pltpu.SMEM if i in smem else pltpu.HBM if i in unread else pltpu.VMEM)
    many = isinstance(out_shape, tuple)
    vmem = pl.BlockSpec(memory_space=pltpu.VMEM)
    return pl.pallas_call(
        body,
        out_shape=out_shape,
        in_specs=[spec(i) for i in range(len(args))],
        out_specs=tuple(vmem for _ in out_shape) if many else vmem,
        compiler_params=pltpu.CompilerParams(vmem_limit_bytes=8 * 1024 * 1024),
    )(*args)


def dot(a, b, dims):
    return lax.dot_general(a, b, (dims, ((), ())), preferred_element_type=F32)


def pack(rows):
    tiles = []
    for row in rows:
        n = row.shape[1] // LANES
        tiles += [row[:, q * LANES : (q + 1) * LANES] for q in range(n)]
        tiles += [jnp.zeros((8 - n, LANES), F32)]
    return jnp.concatenate(tiles, axis=0)


def unpack(tile, n):
    return jnp.concatenate([tile[q : q + 1] for q in range(n)], axis=1)


def order_of(nz):
    first = [(who, k) for k in range(1, nz // 2) for who in (0, 1)] + [(0, nz // 2), (0, 0)]
    return first + [(1 - who, -k) for who, k in first]


def row_at(block, nz, part):
    who, k = block
    c, z = lax.axis_index("c"), lax.axis_index("z")
    core = c if who == 0 else 1 - c
    step = k * (1 - 2 * c)
    return pl.multiple_of((core * nz + lax.rem(z + step + nz, nz)) * part, 16)


def tall(rows):
    return jnp.concatenate(rows + [rows[-1]] * (8 - len(rows)), axis=0).T


def logits_kernel(nz, ins, held, outs, sender, column, stat):
    scale, pairs, txt, images = ins
    logits, row_out, packed = held
    rows, cols = logits.shape
    part = rows // (NC * nz)
    s = scale[0]
    count = len(images.started)
    txt.start_part(0)
    for i in range(count):
        images.start_part(i)
    for i in range(1, len(txt.started)):
        txt.start_part(i)
    column[...] = tall([unpack(pairs.get(), rows // LANES)])
    for i, n in enumerate(range(0, cols, 256)):
        txt.part(i)
        for j, m in enumerate((0, rows // 2)):
            if i == 0:
                for k in range(j * count // 2, (j + 1) * count // 2):
                    images.part(k)
            block = dot(images.ref[m : m + rows // 2, :], txt.ref[n : n + 256, :], ((1,), (1,)))
            logits[m : m + rows // 2, n : n + 256] = s * block
        sender.send(logits.at[:, n : n + 256], outs[0].at[:, n : n + 256])

    def fold(x):
        return x.reshape(part // 8, 8, cols)

    col_top = jnp.full((8, cols), -jnp.inf, F32)
    col_pos = jnp.zeros((8, cols), F32)
    lane = lax.broadcasted_iota(jnp.int32, (part, LANES), 1)
    for i, block in enumerate(order_of(nz)):
        x = logits[i * part : (i + 1) * part, :]
        col_top = jnp.maximum(col_top, jnp.max(fold(x), axis=0))
        at = pl.ds(row_at(block, nz, part), part)
        hit = lax.broadcasted_iota(jnp.int32, x.shape, 1) == column[at, 0:1].astype(jnp.int32)
        paired = jnp.where(hit, x, 0.0)
        col_pos += jnp.sum(fold(paired), axis=0)
        pos = jnp.sum(paired, axis=1, keepdims=True)
        top = jnp.max(x, axis=1, keepdims=True)
        e = jnp.exp(x - top)
        total = jnp.sum(e, axis=1, keepdims=True)
        mean = jnp.sum(e * x, axis=1, keepdims=True) / total
        lse = top + jnp.log(total)
        stat[at, :] = jnp.where(lane == 0, lse, jnp.where(lane == 1, mean, jnp.where(lane == 2, pos, 0.0)))
    flat = stat[...].T
    row_out[...] = pack([flat[0:1], flat[1:2], flat[2:3]])
    sender.send(row_out, outs[1])

    top = jnp.max(col_top, axis=0, keepdims=True)
    total = moment = jnp.zeros((8, cols), F32)
    for i in range(NC * nz):
        x = logits[i * part : (i + 1) * part, :]
        e = jnp.exp(x - top)
        total += jnp.sum(fold(e), axis=0)
        moment += jnp.sum(fold(e * x), axis=0)
    total = jnp.sum(total, axis=0, keepdims=True)
    moment = jnp.sum(moment, axis=0, keepdims=True)
    pos = jnp.sum(col_pos, axis=0, keepdims=True)
    packed[:24, :] = pack([top + jnp.log(total), moment / total, pos])
    packed[24:, :] = jnp.zeros((packed.shape[0] - 24, LANES), F32)
    for p in range(outs[2].shape[0]):
        sender.send(packed, outs[2].at[p])


def merge(got):
    lse = [x[0:8, :] for x in got]
    top = functools.reduce(jnp.maximum, lse)
    weight = [jnp.exp(x - top) for x in lse]
    total = sum(weight)
    mean = sum(w * x[8:16, :] for w, x in zip(weight, got)) / total
    return top + jnp.log(total), mean, sum(x[16:24, :] for x in got)


def total_of(x):
    return jnp.sum(jnp.sum(x, axis=1, keepdims=True), axis=0, keepdims=True)


def split_tail(total, size):
    high = total.astype(BF16)
    rest = total - high.astype(F32)
    middle = rest.astype(BF16)
    low = (rest - middle.astype(F32)).astype(BF16)
    lane = lax.broadcasted_iota(jnp.int32, (size, LANES), 1)
    tail = jnp.where(lane == 0, high.astype(F32), jnp.where(lane == 1, middle.astype(F32), low.astype(F32)))
    return tail.astype(BF16)


def tail_of(ref, embed):
    tail = ref[0:16, embed:].astype(F32)[0:8]
    lane = lax.broadcasted_iota(jnp.int32, tail.shape, 1)
    return jnp.sum(jnp.where(lane < 3, tail, 0.0), axis=1, keepdims=True)


def grad_kernel(count, nz, ins, held, outs, sender, column, grad, turned):
    scale, col_got, chip, across, mine, theirs, pairs, logits, txt, images = ins
    text, first, row_loss, col_loss, sums, send = held
    rows, cols = grad.shape
    half = rows // 2
    peers, embed = text.shape[0], images.ref.shape[1]
    part = rows // (NC * nz)
    s = scale[0]
    used = lax.broadcasted_iota(jnp.int32, (8, LANES), 0) < count
    row_lse, row_mean, row_pos = merge([r.get()[...] for r in (chip, across, mine, theirs)])
    row_loss[...] = row_lse - row_pos
    sender.send(row_loss, outs[2])
    row_total = total_of(jnp.where(used, 0.5 * row_mean - row_pos, 0.0))
    col_ref = col_got.get()
    col_lse, col_mean, col_pos = merge([col_ref[p] for p in range(col_ref.shape[0])])
    col_loss[...] = col_lse - col_pos
    sender.send(col_loss, outs[3])
    col_total = total_of(jnp.where(used, 0.5 * col_mean, 0.0))
    sums[...] = jnp.broadcast_to(col_total, sums.shape)
    sender.send(sums, outs[4])
    send[:, embed:] = split_tail(jnp.broadcast_to(col_total, (1, LANES)), half)
    sender.send(send.at[:, embed:], outs[5].at[:, embed:])
    last = embed // LANES * part
    text[:, last:, :] = jnp.broadcast_to(
        split_tail(jnp.broadcast_to(row_total, (1, LANES)), text.shape[1] - last)[None],
        (peers, text.shape[1] - last, LANES),
    )
    sender.send(text.at[:, last:], outs[0].at[:, last:])
    flat = unpack(col_lse, count)
    column[...] = tall([unpack(row_lse, count), unpack(pairs.get(), count)])

    for i, block in enumerate(order_of(nz)):
        logits.part(i)
        if i == nz // 2:
            txt.start()
        if i == nz:
            images.start()
        x = logits.ref[i * part : (i + 1) * part, :]
        at = pl.ds(row_at(block, nz, part), part)
        hit = lax.broadcasted_iota(jnp.int32, x.shape, 1) == column[at, 1:2].astype(jnp.int32)
        value = 0.5 * (jnp.exp(x - column[at, 0:1]) + jnp.exp(x - flat)) - jnp.where(hit, 1.0, 0.0)
        grad[i * part : (i + 1) * part, :] = (s * value).astype(BF16)
    first[...] = grad[:half, :]
    sender.send(first, outs[1])

    for i, n in enumerate(range(0, embed, 256)):
        txt.part(i)
        send[:, n : n + 256] = dot(grad[half:, :], txt.ref[:, n : n + 256], ((1,), (0,))).astype(BF16)
        sender.send(send.at[:, n : n + 256], outs[5].at[:, n : n + 256])
    turned[...] = grad[...].T
    images = images.get()
    for n in range(0, embed, 256):
        block = dot(turned[...], images[:, n : n + 256], ((1,), (0,))).reshape(peers, part, 256)
        at = n // LANES * part
        text[:, at : at + part, :] = block[:, :, :LANES].astype(BF16)
        text[:, at + part : at + 2 * part, :] = block[:, :, LANES:].astype(BF16)
        sender.send(text.at[:, at : at + 2 * part], outs[0].at[:, at : at + 2 * part])


def image_kernel(ins, held, outs, sender):
    sums, grad, txt, received = ins
    embed = txt.ref.shape[1]
    cuts = range(0, embed, 256)
    grad = grad.get()
    for i, n in enumerate(cuts):
        txt.part(i)
        received.part(i)
        block = dot(grad[...], txt.ref[:, n : n + 256], ((1,), (0,)))
        block += received.ref[:, n : n + 256].astype(F32)
        at = 0
        for ref in held:
            size = ref.shape[0]
            ref[:, n : n + 256] = block[at : at + size].astype(ref.dtype)
            at += size
    received.part(len(cuts))
    total = sums.get()[0:1, :] + tail_of(received.ref, embed)[0:1]
    for ref, out in zip(held, outs):
        size = ref.shape[0]
        ref[:, embed:] = split_tail(total, size) if ref.dtype == BF16 else jnp.broadcast_to(total, (size, LANES))
        sender.send(ref, out)


def forward_kernel(ins, held, outs, sender):
    own, near_one, far_one = ins
    (out,) = held
    own, near_one, far_one = own.get(), near_one.get(), far_one.get()
    part, embed = own.shape[0] // NC, own.shape[1] - LANES
    total = own[:, :embed] + near_one[:, :embed].astype(F32)
    out[:part, :embed] = (total[:part] + far_one[:, :embed].astype(F32)).astype(BF16)
    out[part:, :embed] = total[part:].astype(BF16)
    across = jnp.where(lax.axis_index("c") == 0, 1.0, 0.0) * tail_of(far_one, embed)
    tail = own[0:1, embed:] + tail_of(near_one, embed)[0:1] + across[0:1]
    out[:, embed:] = split_tail(tail, NC * part)
    sender.send(out, outs[0])


def chip_sum_kernel(own, one, two, *refs):
    keep, send = refs[-2], refs[-1]
    part, embed = own.shape[0], own.shape[1] - LANES
    total = one[:, :embed].astype(F32) + two[:, :embed].astype(F32)
    tail = tail_of(one, embed) + tail_of(two, embed)
    send[:, :embed] = total[part:]
    send[:, embed:] = jnp.zeros((part, LANES), F32)
    send[0:8, embed:] = jnp.broadcast_to(tail, (8, LANES))
    keep[:, :embed] = own[:, :embed] + total[:part]
    keep[:, embed:] = own[:, embed:]
    keep[0:8, embed:] = tail + own[0:8, embed:]


def image_sum_kernel(scale, keep, received, others, out, temp):
    embed = out.shape[1]
    out[...] = keep[:, :embed] + received[:, :embed]
    total = keep[0:8, embed:] + received[0:8, embed:] + others[...]
    temp[...] = total[0:1, 0:1] * scale[0]


def text_sum_kernel(got, unread, out, rows_total):
    part = out.shape[0]
    total = got[0].astype(F32)
    for p in range(1, got.shape[0]):
        total = total + got[p].astype(F32)
    for i in range(out.shape[1] // LANES):
        out[:, i * LANES : (i + 1) * LANES] = total[i * part : (i + 1) * part]
    tail = total[out.shape[1] // LANES * part :][0:8]
    lane = lax.broadcasted_iota(jnp.int32, tail.shape, 1)
    tail = jnp.sum(jnp.where(lane < 3, tail, 0.0), axis=1, keepdims=True)
    rows_total[...] = jnp.broadcast_to(tail, rows_total.shape)


def local(image_embed, text_embed, pair_col, log_scale):
    part, embed = image_embed.shape
    peers = NY * NX
    nz = lax.axis_size("z")
    half = nz * part
    rows, cols = NC * half, peers * part
    count = rows // LANES
    batch = peers * rows
    c = lax.axis_index("c")
    z = lax.axis_index("z")
    scale = jnp.exp(log_scale)
    scale1 = scale[None]
    sds = jax.ShapeDtypeStruct
    vmem = pltpu.VMEM
    last = nz // 2

    def swap(x):
        return lax.ppermute(x, "c", SWAP)

    def ahead(x, k):
        pairs = [((i + k) % nz, i) for i in range(nz)]
        return lax.ppermute(x, CZ, pairs + [(nz + i, nz + (i + k) % nz) for i in range(nz)])

    def onward(x, k):
        pairs = [(i, (i + k) % nz) for i in range(nz)]
        return lax.ppermute(x, CZ, pairs + [(nz + (i + k) % nz, nz + i) for i in range(nz)])

    spread = jnp.broadcast_to(text_embed[None], (peers, part, embed))
    txt = lax.all_to_all(spread, XY, 0, 0).reshape(cols, embed)
    partner = swap(image_embed)
    chip = jnp.concatenate([image_embed, partner])
    got = [ahead(chip, 1), ahead(chip, 2)]
    got += [ahead(got[1], 1), ahead(got[1][:part], 2)]
    images = got + [image_embed] + [swap(x) for x in got] + [partner]

    rem = pair_col % (cols * NC)
    block = rem // part
    ours = pair_col // (cols * NC) == z
    place = (block // NC * part + rem % part).astype(F32)
    mine = jnp.where(ours & (block % NC == c), place, -1.0)
    theirs = swap(jnp.where(ours & (block % NC == 1 - c), place, -1.0))
    pairs = jnp.where(c == 0, jnp.concatenate([mine, theirs]), jnp.concatenate([theirs, mine]))
    pairs = jnp.pad(pairs, (0, 8 * LANES - rows)).reshape(8, LANES)

    work = 2 * rows * cols * embed
    tile, pad = sds((24, LANES), F32), sds((8, LANES), F32)
    message = sds((MESSAGE, LANES), F32)
    logits, stat, msg = call(
        functools.partial(logits_kernel, nz),
        (sds((rows, cols), F32), tile, sds((peers, MESSAGE, LANES), F32)),
        scale1,
        pairs,
        txt,
        *images,
        flops=work,
        smem=(0,),
        cuts={2: (0, 256)},
        joined=3,
        later=(2, 3),
        held=(None, None, message),
        sends=1 + cols // 256 + peers,
        scratch=[vmem((rows, 8), F32), vmem((rows, LANES), F32)],
    )
    col_got = lax.all_to_all(msg, XY, 0, 0)
    chip_stat = jnp.concatenate(merge([stat, swap(stat)]))
    stats = [ahead(chip_stat, k) for k in range(last, 0, -1)]
    merged = jnp.concatenate(merge(stats[1:]))

    wide = embed + LANES
    high = embed // LANES * part + 16
    text_term, first, row_loss, col_loss, sums, send = call(
        functools.partial(grad_kernel, count, nz),
        (sds((peers, high, LANES), BF16), sds((half, cols), BF16), pad, pad, pad, sds((half, wide), BF16)),
        scale1,
        col_got,
        chip_stat,
        stats[0],
        merged,
        swap(merged),
        pairs,
        logits,
        txt,
        *images,
        flops=2 * work,
        smem=(0,),
        cuts={7: (0, part), 8: (1, 256)},
        joined=9,
        later=(8, 9),
        scratch=[vmem((rows, 8), F32), vmem((rows, cols), BF16), vmem((cols, rows), BF16)],
    )
    received = swap(send)
    text_got = lax.all_to_all(text_term, XY, 0, 0)
    chip_rows = sds((NC * part, wide), BF16)
    one, two, three, four, own = call(
        image_kernel,
        (chip_rows, sds((NC * part, wide), F32), chip_rows, sds((part, wide), BF16), sds((part, wide), F32)),
        sums,
        first,
        txt,
        received,
        flops=work // 2,
        cuts={2: (1, 256), 3: (1, 256)},
        spare=6 << 20,
    )
    two = call(forward_kernel, chip_rows, two, onward(three, 1), onward(four, 2), spare=VMEM_BYTES // 2)
    row_loss = lax.dynamic_slice(row_loss, (c * (count // NC), 0), (count // NC, LANES)).reshape(-1)
    col_loss = col_loss[:count].reshape(peers, 1, part)
    other = swap(col_loss)
    col_loss = jnp.where(
        c == 0, jnp.concatenate([col_loss, other], 1), jnp.concatenate([other, col_loss], 1)
    ).reshape(-1)
    keep, send = small(
        chip_sum_kernel,
        (sds((part, wide), F32), sds((part, wide), F32)),
        own,
        onward(one, 1),
        onward(two, 2),
        row_loss,
        col_loss,
        unread=(3, 4),
    )
    grad_text, row_total = small(text_sum_kernel, (sds((part, embed), F32), pad), text_got, send, unread=(1,))
    grad_image, temp = small(
        image_sum_kernel,
        (sds((part, embed), F32), sds((1, 1), F32)),
        jnp.full((1,), 1.0 / batch, F32),
        keep,
        swap(send),
        row_total,
        smem=(0,),
    )
    return (row_loss, col_loss, grad_image, grad_text, temp[0, 0])


def solution(mesh):
    nz = mesh.shape["txt"]
    grid = Mesh(mesh.devices.reshape(NY, NX, NC, nz), ("y", "x", "c", "z"))
    images, texts = ("y", "x", "c", "z"), ("z", "y", "x", "c")
    in_specs = (P(images, None), P(texts, None), P(("y", "x", "c")), P())
    out_specs = (P(("y", "x", "c")), P("z"), P(images, None), P(texts, None), P())
    return jax.shard_map(local, mesh=grid, in_specs=in_specs, out_specs=out_specs, check_vma=False)
```

```python
import functools

import jax
import jax.numpy as jnp
from jax import lax
from jax.experimental import pallas as pl
from jax.experimental.pallas import tpu as pltpu
from jax.sharding import Mesh, PartitionSpec as P

NY, NX, NC = 4, 4, 2
XY = ("x", "y")
CZ = ("c", "z")
SWAP = [(0, 1), (1, 0)]
LANES = 128
VMEM_BYTES = 64 * 1024 * 1024
MESSAGE = 48
SPARE = 1048576
F32 = jnp.float32
BF16 = jnp.bfloat16


class Loaded:
    def __init__(self, source, ref, sems, cut):
        self.ref = ref
        self.started = []
        axis, size = cut
        for i, at in enumerate(range(0, ref.shape[axis], size)):
            window = (slice(None),) * axis + (slice(at, at + size),)
            self.started.append(pltpu.make_async_copy(source.at[window], ref.at[window], sems.at[i]))

    def start(self):
        for copy in self.started:
            copy.start()

    def start_part(self, i):
        self.started[i].start()

    def part(self, i):
        self.started[i].wait()

    def get(self):
        for i in range(len(self.started)):
            self.part(i)
        return self.ref


class Joined(Loaded):
    def __init__(self, sources, ref, sems):
        self.ref = ref
        self.started = []
        at = 0
        for i, source in enumerate(sources):
            size = source.shape[0]
            self.started.append(pltpu.make_async_copy(source, ref.at[at : at + size], sems.at[i]))
            at += size


class Sender:
    def __init__(self, sems):
        self.sems = sems
        self.started = []

    def send(self, source, target):
        copy = pltpu.make_async_copy(source, target, self.sems.at[len(self.started)])
        copy.start()
        self.started.append(copy)

    def finish(self):
        for copy in self.started:
            copy.wait()


def call(body, out_shape, *args, flops=0, smem=(), scratch=(), cuts=(), joined=None, held=None, sends=16, spare=0, later=()):
    many = isinstance(out_shape, tuple)
    shapes = out_shape if many else (out_shape,)
    held = [x if held is None or held[i] is None else held[i] for i, x in enumerate(shapes)]
    cuts = dict(cuts)
    joined = len(args) if joined is None else joined
    arrays = [i for i in range(joined) if i not in smem]
    plan = [cuts.get(i, (0, args[i].shape[0])) for i in arrays]
    counts = [-(-args[i].shape[axis] // size) for i, (axis, size) in zip(arrays, plan)]
    buffers_of = [pltpu.VMEM(args[i].shape, args[i].dtype) for i in arrays]
    if joined < len(args):
        counts.append(len(args) - joined)
        last = args[-1]
        buffers_of.append(pltpu.VMEM((sum(a.shape[0] for a in args[joined:]), last.shape[1]), last.dtype))

    def kernel(*refs):
        ins, refs = refs[: len(args)], refs[len(args) :]
        outs, refs = refs[: len(shapes)], refs[len(shapes) :]
        buffers, refs = refs[: len(buffers_of)], refs[len(buffers_of) :]
        kept, refs = refs[: len(held)], refs[len(held) :]
        in_sems, refs = refs[: len(counts)], refs[len(counts) :]
        out_sems, refs = refs[0], refs[1:]
        given = list(ins[:joined])
        for j, i in enumerate(arrays):
            given[i] = Loaded(ins[i], buffers[j], in_sems[j], plan[j])
            if i not in later:
                given[i].start()
        if joined < len(args):
            given.append(Joined(ins[joined:], buffers[-1], in_sems[-1]))
            if joined not in later:
                given[-1].start()
        sender = Sender(out_sems)
        body(given, kept, outs, sender, *refs)
        sender.finish()

    far = pl.BlockSpec(memory_space=pl.ANY if spare else pltpu.HBM)
    scalars = pl.BlockSpec(memory_space=pltpu.SMEM)
    size = sum(a.size * a.dtype.itemsize for a in args)
    return pl.pallas_call(
        kernel,
        out_shape=out_shape,
        in_specs=[scalars if i in smem else far for i in range(len(args))],
        out_specs=tuple(far for _ in shapes) if many else far,
        scratch_shapes=[
            *buffers_of,
            *[pltpu.VMEM(x.shape, x.dtype) for x in held],
            *[pltpu.SemaphoreType.DMA((n,)) for n in counts],
            pltpu.SemaphoreType.DMA((sends,)),
            *scratch,
        ],
        cost_estimate=pl.CostEstimate(flops=flops, bytes_accessed=size, transcendentals=0),
        compiler_params=pltpu.CompilerParams(vmem_limit_bytes=VMEM_BYTES - spare),
    )(*args)


def small(body, out_shape, *args, smem=(), unread=()):
    spec = lambda i: pl.BlockSpec(memory_space=pltpu.SMEM if i in smem else pltpu.HBM if i in unread else pltpu.VMEM)
    many = isinstance(out_shape, tuple)
    vmem = pl.BlockSpec(memory_space=pltpu.VMEM)
    return pl.pallas_call(
        body,
        out_shape=out_shape,
        in_specs=[spec(i) for i in range(len(args))],
        out_specs=tuple(vmem for _ in out_shape) if many else vmem,
        compiler_params=pltpu.CompilerParams(vmem_limit_bytes=8 * 1024 * 1024),
    )(*args)


def dot(a, b, dims):
    return lax.dot_general(a, b, (dims, ((), ())), preferred_element_type=F32)


def pack(rows):
    tiles = []
    for row in rows:
        n = row.shape[1] // LANES
        tiles += [row[:, q * LANES : (q + 1) * LANES] for q in range(n)]
        tiles += [jnp.zeros((8 - n, LANES), F32)]
    return jnp.concatenate(tiles, axis=0)


def unpack(tile, n):
    return jnp.concatenate([tile[q : q + 1] for q in range(n)], axis=1)


def order_of(nz):
    first = [(who, k) for k in range(1, nz // 2) for who in (0, 1)] + [(0, nz // 2), (0, 0)]
    return first + [(1 - who, -k) for who, k in first]


def row_at(block, nz, part):
    who, k = block
    c, z = lax.axis_index("c"), lax.axis_index("z")
    core = c if who == 0 else 1 - c
    step = k * (1 - 2 * c)
    return pl.multiple_of((core * nz + lax.rem(z + step + nz, nz)) * part, 16)


def tall(rows):
    return jnp.concatenate(rows + [rows[-1]] * (8 - len(rows)), axis=0).T


def spread_kernel(ins, held, outs, sender):
    for p in range(outs[0].shape[0]):
        if p == 0:
            ins[0].get()
        sender.send(ins[0].ref, outs[0].at[p])


def logits_kernel(nz, ins, held, outs, sender, column, stat):
    scale, pairs, txt, images = ins
    logits, row_out, packed = held
    rows, cols = logits.shape
    part = rows // (NC * nz)
    s = scale[0]
    count = len(images.started)
    txt.start_part(0)
    for i in range(count):
        images.start_part(i)
    for i in range(1, len(txt.started)):
        txt.start_part(i)
    column[...] = tall([unpack(pairs.get(), rows // LANES)])
    for i, n in enumerate(range(0, cols, 256)):
        txt.part(i)
        for j, m in enumerate((0, rows // 2)):
            if i == 0:
                for k in range(j * count // 2, (j + 1) * count // 2):
                    images.part(k)
            block = dot(images.ref[m : m + rows // 2, :], txt.ref[n : n + 256, :], ((1,), (1,)))
            logits[m : m + rows // 2, n : n + 256] = s * block
        sender.send(logits.at[:, n : n + 256], outs[0].at[:, n : n + 256])

    def fold(x):
        return x.reshape(part // 8, 8, cols)

    col_top = jnp.full((8, cols), -jnp.inf, F32)
    col_pos = jnp.zeros((8, cols), F32)
    lane = lax.broadcasted_iota(jnp.int32, (part, LANES), 1)
    for i, block in enumerate(order_of(nz)):
        x = logits[i * part : (i + 1) * part, :]
        col_top = jnp.maximum(col_top, jnp.max(fold(x), axis=0))
        at = pl.ds(row_at(block, nz, part), part)
        hit = lax.broadcasted_iota(jnp.int32, x.shape, 1) == column[at, 0:1].astype(jnp.int32)
        paired = jnp.where(hit, x, 0.0)
        col_pos += jnp.sum(fold(paired), axis=0)
        pos = jnp.sum(paired, axis=1, keepdims=True)
        top = jnp.max(x, axis=1, keepdims=True)
        e = jnp.exp(x - top)
        total = jnp.sum(e, axis=1, keepdims=True)
        mean = jnp.sum(e * x, axis=1, keepdims=True) / total
        lse = top + jnp.log(total)
        stat[at, :] = jnp.where(lane == 0, lse, jnp.where(lane == 1, mean, jnp.where(lane == 2, pos, 0.0)))
    flat = stat[...].T
    row_out[...] = pack([flat[0:1], flat[1:2], flat[2:3]])
    sender.send(row_out, outs[1])

    top = jnp.max(col_top, axis=0, keepdims=True)
    total = moment = jnp.zeros((8, cols), F32)
    for i in range(NC * nz):
        x = logits[i * part : (i + 1) * part, :]
        e = jnp.exp(x - top)
        total += jnp.sum(fold(e), axis=0)
        moment += jnp.sum(fold(e * x), axis=0)
    total = jnp.sum(total, axis=0, keepdims=True)
    moment = jnp.sum(moment, axis=0, keepdims=True)
    pos = jnp.sum(col_pos, axis=0, keepdims=True)
    packed[:24, :] = pack([top + jnp.log(total), moment / total, pos])
    packed[24:, :] = jnp.zeros((packed.shape[0] - 24, LANES), F32)
    for p in range(outs[2].shape[0]):
        sender.send(packed, outs[2].at[p])


def merge(got):
    lse = [x[0:8, :] for x in got]
    top = functools.reduce(jnp.maximum, lse)
    weight = [jnp.exp(x - top) for x in lse]
    total = sum(weight)
    mean = sum(w * x[8:16, :] for w, x in zip(weight, got)) / total
    return top + jnp.log(total), mean, sum(x[16:24, :] for x in got)


def total_of(x):
    return jnp.sum(jnp.sum(x, axis=1, keepdims=True), axis=0, keepdims=True)


def split_tail(total, size):
    high = total.astype(BF16)
    rest = total - high.astype(F32)
    middle = rest.astype(BF16)
    low = (rest - middle.astype(F32)).astype(BF16)
    lane = lax.broadcasted_iota(jnp.int32, (size, LANES), 1)
    tail = jnp.where(lane == 0, high.astype(F32), jnp.where(lane == 1, middle.astype(F32), low.astype(F32)))
    return tail.astype(BF16)


def tail_of(ref, embed):
    tail = ref[0:16, embed:].astype(F32)[0:8]
    lane = lax.broadcasted_iota(jnp.int32, tail.shape, 1)
    return jnp.sum(jnp.where(lane < 3, tail, 0.0), axis=1, keepdims=True)


def grad_kernel(count, nz, ins, held, outs, sender, column, grad, turned):
    scale, col_got, chip, across, mine, theirs, pairs, logits, txt, images = ins
    text, first, row_loss, col_loss, sums, send = held
    rows, cols = grad.shape
    half = rows // 2
    peers, embed = text.shape[0], images.ref.shape[1]
    part = rows // (NC * nz)
    s = scale[0]
    used = lax.broadcasted_iota(jnp.int32, (8, LANES), 0) < count
    row_lse, row_mean, row_pos = merge([r.get()[...] for r in (chip, across, mine, theirs)])
    row_loss[...] = row_lse - row_pos
    sender.send(row_loss, outs[2])
    row_total = total_of(jnp.where(used, 0.5 * row_mean - row_pos, 0.0))
    col_ref = col_got.get()
    col_lse, col_mean, col_pos = merge([col_ref[p] for p in range(col_ref.shape[0])])
    col_loss[...] = col_lse - col_pos
    sender.send(col_loss, outs[3])
    col_total = total_of(jnp.where(used, 0.5 * col_mean, 0.0))
    sums[...] = jnp.broadcast_to(col_total, sums.shape)
    sender.send(sums, outs[4])
    send[:, embed:] = split_tail(jnp.broadcast_to(col_total, (1, LANES)), half)
    sender.send(send.at[:, embed:], outs[5].at[:, embed:])
    last = embed // LANES * part
    text[:, last:, :] = jnp.broadcast_to(
        split_tail(jnp.broadcast_to(row_total, (1, LANES)), text.shape[1] - last)[None],
        (peers, text.shape[1] - last, LANES),
    )
    sender.send(text.at[:, last:], outs[0].at[:, last:])
    flat = unpack(col_lse, count)
    column[...] = tall([unpack(row_lse, count), unpack(pairs.get(), count)])

    for i, block in enumerate(order_of(nz)):
        logits.part(i)
        if i == nz // 2:
            txt.start()
        if i == nz:
            images.start()
        x = logits.ref[i * part : (i + 1) * part, :]
        at = pl.ds(row_at(block, nz, part), part)
        hit = lax.broadcasted_iota(jnp.int32, x.shape, 1) == column[at, 1:2].astype(jnp.int32)
        value = 0.5 * (jnp.exp(x - column[at, 0:1]) + jnp.exp(x - flat)) - jnp.where(hit, 1.0, 0.0)
        grad[i * part : (i + 1) * part, :] = (s * value).astype(BF16)
    first[...] = grad[:half, :]
    sender.send(first, outs[1])

    for i, n in enumerate(range(0, embed, 256)):
        txt.part(i)
        send[:, n : n + 256] = dot(grad[half:, :], txt.ref[:, n : n + 256], ((1,), (0,))).astype(BF16)
        sender.send(send.at[:, n : n + 256], outs[5].at[:, n : n + 256])
    turned[...] = grad[...].T
    images = images.get()
    for n in range(0, embed, 256):
        block = dot(turned[...], images[:, n : n + 256], ((1,), (0,))).reshape(peers, part, 256)
        at = n // LANES * part
        text[:, at : at + part, :] = block[:, :, :LANES].astype(BF16)
        text[:, at + part : at + 2 * part, :] = block[:, :, LANES:].astype(BF16)
        sender.send(text.at[:, at : at + 2 * part], outs[0].at[:, at : at + 2 * part])


def image_kernel(ins, held, outs, sender):
    sums, grad, txt, received = ins
    embed = txt.ref.shape[1]
    cuts = range(0, embed, 256)
    grad = grad.get()
    for i, n in enumerate(cuts):
        txt.part(i)
        received.part(i)
        block = dot(grad[...], txt.ref[:, n : n + 256], ((1,), (0,)))
        block += received.ref[:, n : n + 256].astype(F32)
        at = 0
        for ref in held:
            size = ref.shape[0]
            ref[:, n : n + 256] = block[at : at + size].astype(ref.dtype)
            at += size
    received.part(len(cuts))
    total = sums.get()[0:1, :] + tail_of(received.ref, embed)[0:1]
    for ref, out in zip(held, outs):
        size = ref.shape[0]
        ref[:, embed:] = split_tail(total, size) if ref.dtype == BF16 else jnp.broadcast_to(total, (size, LANES))
        sender.send(ref, out)


def forward_kernel(ins, held, outs, sender):
    own, near_one, far_one = ins
    (out,) = held
    own, near_one, far_one = own.get(), near_one.get(), far_one.get()
    part, embed = own.shape[0] // NC, own.shape[1] - LANES
    total = own[:, :embed] + near_one[:, :embed].astype(F32)
    out[:part, :embed] = (total[:part] + far_one[:, :embed].astype(F32)).astype(BF16)
    out[part:, :embed] = total[part:].astype(BF16)
    across = jnp.where(lax.axis_index("c") == 0, 1.0, 0.0) * tail_of(far_one, embed)
    tail = own[0:1, embed:] + tail_of(near_one, embed)[0:1] + across[0:1]
    out[:, embed:] = split_tail(tail, NC * part)
    sender.send(out, outs[0])


def chip_sum_kernel(own, one, two, *refs):
    keep, send = refs[-2], refs[-1]
    part, embed = own.shape[0], own.shape[1] - LANES
    total = one[:, :embed].astype(F32) + two[:, :embed].astype(F32)
    tail = tail_of(one, embed) + tail_of(two, embed)
    send[:, :embed] = total[part:]
    send[:, embed:] = jnp.zeros((part, LANES), F32)
    send[0:8, embed:] = jnp.broadcast_to(tail, (8, LANES))
    keep[:, :embed] = own[:, :embed] + total[:part]
    keep[:, embed:] = own[:, embed:]
    keep[0:8, embed:] = tail + own[0:8, embed:]


def image_sum_kernel(scale, keep, received, others, out, temp):
    embed = out.shape[1]
    out[...] = keep[:, :embed] + received[:, :embed]
    total = keep[0:8, embed:] + received[0:8, embed:] + others[...]
    temp[...] = total[0:1, 0:1] * scale[0]


def text_sum_kernel(got, unread, out, rows_total):
    part = out.shape[0]
    total = got[0].astype(F32)
    for p in range(1, got.shape[0]):
        total = total + got[p].astype(F32)
    for i in range(out.shape[1] // LANES):
        out[:, i * LANES : (i + 1) * LANES] = total[i * part : (i + 1) * part]
    tail = total[out.shape[1] // LANES * part :][0:8]
    lane = lax.broadcasted_iota(jnp.int32, tail.shape, 1)
    tail = jnp.sum(jnp.where(lane < 3, tail, 0.0), axis=1, keepdims=True)
    rows_total[...] = jnp.broadcast_to(tail, rows_total.shape)


def local(image_embed, text_embed, pair_col, log_scale):
    part, embed = image_embed.shape
    peers = NY * NX
    nz = lax.axis_size("z")
    half = nz * part
    rows, cols = NC * half, peers * part
    count = rows // LANES
    batch = peers * rows
    c = lax.axis_index("c")
    z = lax.axis_index("z")
    scale = jnp.exp(log_scale)
    scale1 = scale[None]
    sds = jax.ShapeDtypeStruct
    vmem = pltpu.VMEM
    last = nz // 2

    def swap(x):
        return lax.ppermute(x, "c", SWAP)

    def ahead(x, k):
        pairs = [((i + k) % nz, i) for i in range(nz)]
        return lax.ppermute(x, CZ, pairs + [(nz + i, nz + (i + k) % nz) for i in range(nz)])

    def onward(x, k):
        pairs = [(i, (i + k) % nz) for i in range(nz)]
        return lax.ppermute(x, CZ, pairs + [(nz + (i + k) % nz, nz + i) for i in range(nz)])

    spread = call(spread_kernel, sds((peers, part, embed), BF16), text_embed, flops=1 << 34, held=(sds((8, LANES), BF16),))
    txt = lax.all_to_all(spread, XY, 0, 0).reshape(cols, embed)
    partner = swap(image_embed)
    chip = jnp.concatenate([image_embed, partner])
    got = [ahead(chip, 1), ahead(chip, 2)]
    got += [ahead(got[1], 1), ahead(got[1][:part], 2)]
    images = got + [image_embed] + [swap(x) for x in got] + [partner]

    rem = pair_col % (cols * NC)
    block = rem // part
    ours = pair_col // (cols * NC) == z
    chip = block // NC
    place = ((chip % NX * NY + chip // NX) * part + rem % part).astype(F32)
    mine = jnp.where(ours & (block % NC == c), place, -1.0)
    theirs = swap(jnp.where(ours & (block % NC == 1 - c), place, -1.0))
    pairs = jnp.where(c == 0, jnp.concatenate([mine, theirs]), jnp.concatenate([theirs, mine]))
    pairs = jnp.pad(pairs, (0, 8 * LANES - rows)).reshape(8, LANES)

    work = 2 * rows * cols * embed
    tile, pad = sds((24, LANES), F32), sds((8, LANES), F32)
    message = sds((MESSAGE, LANES), F32)
    logits, stat, msg = call(
        functools.partial(logits_kernel, nz),
        (sds((rows, cols), F32), tile, sds((peers, MESSAGE, LANES), F32)),
        scale1,
        pairs,
        txt,
        *images,
        flops=work,
        smem=(0,),
        cuts={2: (0, 256)},
        joined=3,
        later=(2, 3),
        held=(None, None, message),
        spare=SPARE,
        sends=1 + cols // 256 + peers,
        scratch=[vmem((rows, 8), F32), vmem((rows, LANES), F32)],
    )
    col_got = lax.all_to_all(msg, XY, 0, 0)
    chip_stat = jnp.concatenate(merge([stat, swap(stat)]))
    stats = [ahead(chip_stat, k) for k in range(last, 0, -1)]
    merged = jnp.concatenate(merge(stats[1:]))

    wide = embed + LANES
    high = embed // LANES * part + 16
    text_term, first, row_loss, col_loss, sums, send = call(
        functools.partial(grad_kernel, count, nz),
        (sds((peers, high, LANES), BF16), sds((half, cols), BF16), pad, pad, pad, sds((half, wide), BF16)),
        scale1,
        col_got,
        chip_stat,
        stats[0],
        merged,
        swap(merged),
        pairs,
        logits,
        txt,
        *images,
        flops=2 * work,
        smem=(0,),
        cuts={7: (0, part), 8: (1, 256)},
        joined=9,
        later=(8, 9),
        spare=SPARE,
        scratch=[vmem((rows, 8), F32), vmem((rows, cols), BF16), vmem((cols, rows), BF16)],
    )
    received = swap(send)
    text_got = lax.all_to_all(text_term, XY, 0, 0)
    chip_rows = sds((NC * part, wide), BF16)
    one, two, three, four, own = call(
        image_kernel,
        (chip_rows, sds((NC * part, wide), F32), chip_rows, sds((part, wide), BF16), sds((part, wide), F32)),
        sums,
        first,
        txt,
        received,
        flops=work // 2,
        cuts={2: (1, 256), 3: (1, 256)},
        spare=VMEM_BYTES // 2,
    )
    two = call(forward_kernel, chip_rows, two, onward(three, 1), onward(four, 2), spare=VMEM_BYTES // 2)
    row_loss = lax.dynamic_slice(row_loss, (c * (count // NC), 0), (count // NC, LANES)).reshape(-1)
    col_loss = jnp.swapaxes(col_loss[:count].reshape(NX, NY, part), 0, 1).reshape(peers, 1, part)
    other = swap(col_loss)
    col_loss = jnp.where(
        c == 0, jnp.concatenate([col_loss, other], 1), jnp.concatenate([other, col_loss], 1)
    ).reshape(-1)
    keep, send = small(
        chip_sum_kernel,
        (sds((part, wide), F32), sds((part, wide), F32)),
        own,
        onward(one, 1),
        onward(two, 2),
        row_loss,
        col_loss,
        unread=(3, 4),
    )
    grad_text, row_total = small(text_sum_kernel, (sds((part, embed), F32), pad), text_got, send, unread=(1,))
    grad_image, temp = small(
        image_sum_kernel,
        (sds((part, embed), F32), sds((1, 1), F32)),
        jnp.full((1,), 1.0 / batch, F32),
        keep,
        swap(send),
        row_total,
        smem=(0,),
    )
    return (row_loss, col_loss, grad_image, grad_text, temp[0, 0])


def solution(mesh):
    nz = mesh.shape["txt"]
    grid = Mesh(mesh.devices.reshape(NY, NX, NC, nz), ("y", "x", "c", "z"))
    images, texts = ("y", "x", "c", "z"), ("z", "y", "x", "c")
    in_specs = (P(images, None), P(texts, None), P(("y", "x", "c")), P())
    out_specs = (P(("y", "x", "c")), P("z"), P(images, None), P(texts, None), P())
    return jax.shard_map(local, mesh=grid, in_specs=in_specs, out_specs=out_specs, check_vma=False)
```

```python
import functools

import jax
import jax.numpy as jnp
from jax import lax
from jax.experimental import pallas as pl
from jax.experimental.pallas import tpu as pltpu
from jax.sharding import Mesh, PartitionSpec as P

NY, NX, NC = 4, 4, 2
CHIP = ("y1", "y0", "x1", "x0")
XY = ("y0", "y1", "x0", "x1")
CZ = ("c", "z")
SWAP = [(0, 1), (1, 0)]
LANES = 128
VMEM_BYTES = 64 * 1024 * 1024
MESSAGE = 48
SPARE = 1048576
F32 = jnp.float32
BF16 = jnp.bfloat16


class Loaded:
    def __init__(self, source, ref, sems, cut):
        self.ref = ref
        self.started = []
        axis, size = cut
        for i, at in enumerate(range(0, ref.shape[axis], size)):
            window = (slice(None),) * axis + (slice(at, at + size),)
            self.started.append(pltpu.make_async_copy(source.at[window], ref.at[window], sems.at[i]))

    def start(self):
        for copy in self.started:
            copy.start()

    def start_part(self, i):
        self.started[i].start()

    def part(self, i):
        self.started[i].wait()

    def get(self):
        for i in range(len(self.started)):
            self.part(i)
        return self.ref


class Joined(Loaded):
    def __init__(self, sources, ref, sems):
        self.ref = ref
        self.started = []
        at = 0
        for i, source in enumerate(sources):
            size = source.shape[0]
            self.started.append(pltpu.make_async_copy(source, ref.at[at : at + size], sems.at[i]))
            at += size


class Sender:
    def __init__(self, sems):
        self.sems = sems
        self.started = []

    def send(self, source, target):
        copy = pltpu.make_async_copy(source, target, self.sems.at[len(self.started)])
        copy.start()
        self.started.append(copy)

    def finish(self):
        for copy in self.started:
            copy.wait()


def call(body, out_shape, *args, flops=0, smem=(), scratch=(), cuts=(), joined=None, held=None, sends=16, spare=0, later=(), fixed=()):
    many = isinstance(out_shape, tuple)
    shapes = out_shape if many else (out_shape,)
    held = [x if held is None or held[i] is None else held[i] for i, x in enumerate(shapes)]
    cuts = dict(cuts)
    joined = len(args) if joined is None else joined
    arrays = [i for i in range(joined) if i not in smem]
    plan = [cuts.get(i, (0, args[i].shape[0])) for i in arrays]
    counts = [-(-args[i].shape[axis] // size) for i, (axis, size) in zip(arrays, plan)]
    buffers_of = [pltpu.VMEM(args[i].shape, args[i].dtype) for i in arrays]
    if joined < len(args):
        counts.append(len(args) - joined)
        last = args[-1]
        buffers_of.append(pltpu.VMEM((sum(a.shape[0] for a in args[joined:]), last.shape[1]), last.dtype))

    def kernel(*refs):
        ins, refs = refs[: len(args)], refs[len(args) :]
        outs, refs = refs[: len(shapes)], refs[len(shapes) :]
        buffers, refs = refs[: len(buffers_of)], refs[len(buffers_of) :]
        kept, refs = refs[: len(held)], refs[len(held) :]
        in_sems, refs = refs[: len(counts)], refs[len(counts) :]
        out_sems, refs = refs[0], refs[1:]
        given = list(ins[:joined])
        for j, i in enumerate(arrays):
            given[i] = Loaded(ins[i], buffers[j], in_sems[j], plan[j])
            if i not in later:
                given[i].start()
        if joined < len(args):
            given.append(Joined(ins[joined:], buffers[-1], in_sems[-1]))
            if joined not in later:
                given[-1].start()
        sender = Sender(out_sems)
        body(given, kept, outs, sender, *refs)
        sender.finish()

    far = pl.BlockSpec(memory_space=pl.ANY if spare else pltpu.HBM)
    scalars = pl.BlockSpec(memory_space=pltpu.SMEM)
    size = sum(a.size * a.dtype.itemsize for a in args)
    return pl.pallas_call(
        kernel,
        out_shape=out_shape,
        in_specs=[
            scalars if i in smem else pl.BlockSpec(memory_space=pltpu.HBM) if i in fixed else far
            for i in range(len(args))
        ],
        out_specs=tuple(far for _ in shapes) if many else far,
        scratch_shapes=[
            *buffers_of,
            *[pltpu.VMEM(x.shape, x.dtype) for x in held],
            *[pltpu.SemaphoreType.DMA((n,)) for n in counts],
            pltpu.SemaphoreType.DMA((sends,)),
            *scratch,
        ],
        cost_estimate=pl.CostEstimate(flops=flops, bytes_accessed=size, transcendentals=0),
        compiler_params=pltpu.CompilerParams(vmem_limit_bytes=VMEM_BYTES - spare),
    )(*args)


def small(body, out_shape, *args, smem=(), unread=()):
    spec = lambda i: pl.BlockSpec(memory_space=pltpu.SMEM if i in smem else pltpu.HBM if i in unread else pltpu.VMEM)
    many = isinstance(out_shape, tuple)
    vmem = pl.BlockSpec(memory_space=pltpu.VMEM)
    return pl.pallas_call(
        body,
        out_shape=out_shape,
        in_specs=[spec(i) for i in range(len(args))],
        out_specs=tuple(vmem for _ in out_shape) if many else vmem,
        compiler_params=pltpu.CompilerParams(vmem_limit_bytes=8 * 1024 * 1024),
    )(*args)


def dot(a, b, dims):
    return lax.dot_general(a, b, (dims, ((), ())), preferred_element_type=F32)


def pack(rows):
    tiles = []
    for row in rows:
        n = row.shape[1] // LANES
        tiles += [row[:, q * LANES : (q + 1) * LANES] for q in range(n)]
        tiles += [jnp.zeros((8 - n, LANES), F32)]
    return jnp.concatenate(tiles, axis=0)


def unpack(tile, n):
    return jnp.concatenate([tile[q : q + 1] for q in range(n)], axis=1)


def order_of(nz):
    first = [(who, k) for k in range(1, nz // 2) for who in (0, 1)] + [(0, nz // 2), (0, 0)]
    return first + [(1 - who, -k) for who, k in first]


def row_at(block, nz, part):
    who, k = block
    c, z = lax.axis_index("c"), lax.axis_index("z")
    core = c if who == 0 else 1 - c
    step = k * (1 - 2 * c)
    return pl.multiple_of((core * nz + lax.rem(z + step + nz, nz)) * part, 16)


def tall(rows):
    return jnp.concatenate(rows + [rows[-1]] * (8 - len(rows)), axis=0).T


def spread_kernel(ins, held, outs, sender):
    for p in range(outs[0].shape[0]):
        if p == 0:
            ins[0].get()
        sender.send(ins[0].ref, outs[0].at[p])


def logits_kernel(nz, ins, held, outs, sender, column, stat):
    scale, pairs, txt, images = ins
    logits, row_out, packed = held
    rows, cols = logits.shape
    part = rows // (NC * nz)
    s = scale[0]
    count = len(images.started)
    txt.start_part(0)
    for i in range(count):
        images.start_part(i)
    for i in range(1, len(txt.started)):
        txt.start_part(i)
    column[...] = tall([unpack(pairs.get(), rows // LANES)])
    for i, n in enumerate(range(0, cols, 256)):
        txt.part(i)
        for j, m in enumerate((0, rows // 2)):
            if i == 0:
                for k in range(j * count // 2, (j + 1) * count // 2):
                    images.part(k)
            block = dot(images.ref[m : m + rows // 2, :], txt.ref[n : n + 256, :], ((1,), (1,)))
            logits[m : m + rows // 2, n : n + 256] = s * block
        sender.send(logits.at[:, n : n + 256], outs[0].at[:, n : n + 256])

    def fold(x):
        return x.reshape(part // 8, 8, cols)

    col_top = jnp.full((8, cols), -jnp.inf, F32)
    col_pos = jnp.zeros((8, cols), F32)
    lane = lax.broadcasted_iota(jnp.int32, (part, LANES), 1)
    for i, block in enumerate(order_of(nz)):
        x = logits[i * part : (i + 1) * part, :]
        col_top = jnp.maximum(col_top, jnp.max(fold(x), axis=0))
        at = pl.ds(row_at(block, nz, part), part)
        hit = lax.broadcasted_iota(jnp.int32, x.shape, 1) == column[at, 0:1].astype(jnp.int32)
        paired = jnp.where(hit, x, 0.0)
        col_pos += jnp.sum(fold(paired), axis=0)
        pos = jnp.sum(paired, axis=1, keepdims=True)
        top = jnp.max(x, axis=1, keepdims=True)
        e = jnp.exp(x - top)
        total = jnp.sum(e, axis=1, keepdims=True)
        mean = jnp.sum(e * x, axis=1, keepdims=True) / total
        lse = top + jnp.log(total)
        stat[at, :] = jnp.where(lane == 0, lse, jnp.where(lane == 1, mean, jnp.where(lane == 2, pos, 0.0)))
    flat = stat[...].T
    row_out[...] = pack([flat[0:1], flat[1:2], flat[2:3]])
    sender.send(row_out, outs[1])

    top = jnp.max(col_top, axis=0, keepdims=True)
    total = moment = jnp.zeros((8, cols), F32)
    for i in range(NC * nz):
        x = logits[i * part : (i + 1) * part, :]
        e = jnp.exp(x - top)
        total += jnp.sum(fold(e), axis=0)
        moment += jnp.sum(fold(e * x), axis=0)
    total = jnp.sum(total, axis=0, keepdims=True)
    moment = jnp.sum(moment, axis=0, keepdims=True)
    pos = jnp.sum(col_pos, axis=0, keepdims=True)
    packed[:24, :] = pack([top + jnp.log(total), moment / total, pos])
    packed[24:, :] = jnp.zeros((packed.shape[0] - 24, LANES), F32)
    for p in range(outs[2].shape[0]):
        sender.send(packed, outs[2].at[p])


def merge(got):
    lse = [x[0:8, :] for x in got]
    top = functools.reduce(jnp.maximum, lse)
    weight = [jnp.exp(x - top) for x in lse]
    total = sum(weight)
    mean = sum(w * x[8:16, :] for w, x in zip(weight, got)) / total
    return top + jnp.log(total), mean, sum(x[16:24, :] for x in got)


def total_of(x):
    return jnp.sum(jnp.sum(x, axis=1, keepdims=True), axis=0, keepdims=True)


def split_tail(total, size):
    high = total.astype(BF16)
    rest = total - high.astype(F32)
    middle = rest.astype(BF16)
    low = (rest - middle.astype(F32)).astype(BF16)
    lane = lax.broadcasted_iota(jnp.int32, (size, LANES), 1)
    tail = jnp.where(lane == 0, high.astype(F32), jnp.where(lane == 1, middle.astype(F32), low.astype(F32)))
    return tail.astype(BF16)


def tail_of(ref, embed):
    tail = ref[0:16, embed:].astype(F32)[0:8]
    lane = lax.broadcasted_iota(jnp.int32, tail.shape, 1)
    return jnp.sum(jnp.where(lane < 3, tail, 0.0), axis=1, keepdims=True)


def grad_kernel(count, nz, ins, held, outs, sender, column, grad, turned):
    scale, col_got, chip, across, mine, theirs, pairs, logits, txt, images = ins
    text, first, row_loss, col_loss, sums, send = held
    rows, cols = grad.shape
    half = rows // 2
    peers, embed = text.shape[0], images.ref.shape[1]
    part = rows // (NC * nz)
    s = scale[0]
    used = lax.broadcasted_iota(jnp.int32, (8, LANES), 0) < count
    row_lse, row_mean, row_pos = merge([r.get()[...] for r in (chip, across, mine, theirs)])
    row_loss[...] = row_lse - row_pos
    sender.send(row_loss, outs[2])
    row_total = total_of(jnp.where(used, 0.5 * row_mean - row_pos, 0.0))
    col_ref = col_got.get()
    col_lse, col_mean, col_pos = merge([col_ref[p] for p in range(col_ref.shape[0])])
    col_loss[...] = col_lse - col_pos
    sender.send(col_loss, outs[3])
    col_total = total_of(jnp.where(used, 0.5 * col_mean, 0.0))
    sums[...] = jnp.broadcast_to(col_total, sums.shape)
    sender.send(sums, outs[4])
    send[:, embed:] = split_tail(jnp.broadcast_to(col_total, (1, LANES)), half)
    sender.send(send.at[:, embed:], outs[5].at[:, embed:])
    last = embed // LANES * part
    text[:, last:, :] = jnp.broadcast_to(
        split_tail(jnp.broadcast_to(row_total, (1, LANES)), text.shape[1] - last)[None],
        (peers, text.shape[1] - last, LANES),
    )
    sender.send(text.at[:, last:], outs[0].at[:, last:])
    flat = unpack(col_lse, count)
    column[...] = tall([unpack(row_lse, count), unpack(pairs.get(), count)])

    for i, block in enumerate(order_of(nz)):
        logits.part(i)
        if i == nz // 2:
            txt.start()
        if i == nz:
            images.start()
        x = logits.ref[i * part : (i + 1) * part, :]
        at = pl.ds(row_at(block, nz, part), part)
        hit = lax.broadcasted_iota(jnp.int32, x.shape, 1) == column[at, 1:2].astype(jnp.int32)
        value = 0.5 * (jnp.exp(x - column[at, 0:1]) + jnp.exp(x - flat)) - jnp.where(hit, 1.0, 0.0)
        grad[i * part : (i + 1) * part, :] = (s * value).astype(BF16)
    sender.send(grad.at[:half, :], outs[1])

    for i, n in enumerate(range(0, embed, 256)):
        txt.part(i)
        send[:, n : n + 256] = dot(grad[half:, :], txt.ref[:, n : n + 256], ((1,), (0,))).astype(BF16)
        sender.send(send.at[:, n : n + 256], outs[5].at[:, n : n + 256])
    turned[...] = grad[...].T
    images = images.get()
    for n in range(0, embed, 256):
        block = dot(turned[...], images[:, n : n + 256], ((1,), (0,))).reshape(peers, part, 256)
        at = n // LANES * part
        text[:, at : at + part, :] = block[:, :, :LANES].astype(BF16)
        text[:, at + part : at + 2 * part, :] = block[:, :, LANES:].astype(BF16)
        sender.send(text.at[:, at : at + 2 * part], outs[0].at[:, at : at + 2 * part])


def image_kernel(ins, held, outs, sender):
    sums, grad, txt, received = ins
    embed = txt.ref.shape[1]
    cuts = range(0, embed, 256)
    grad = grad.get()
    for i, n in enumerate(cuts):
        txt.part(i)
        received.part(i)
        block = dot(grad[...], txt.ref[:, n : n + 256], ((1,), (0,)))
        block += received.ref[:, n : n + 256].astype(F32)
        at = 0
        for ref in held:
            size = ref.shape[0]
            ref[:, n : n + 256] = block[at : at + size].astype(ref.dtype)
            at += size
    received.part(len(cuts))
    total = sums.get()[0:1, :] + tail_of(received.ref, embed)[0:1]
    for ref, out in zip(held, outs):
        size = ref.shape[0]
        ref[:, embed:] = split_tail(total, size) if ref.dtype == BF16 else jnp.broadcast_to(total, (size, LANES))
        sender.send(ref, out)


def forward_kernel(ins, held, outs, sender):
    own, near_one, far_one = ins
    (out,) = held
    own, near_one, far_one = own.get(), near_one.get(), far_one.get()
    part, embed = own.shape[0] // NC, own.shape[1] - LANES
    total = own[:, :embed] + near_one[:, :embed].astype(F32)
    out[:part, :embed] = (total[:part] + far_one[:, :embed].astype(F32)).astype(BF16)
    out[part:, :embed] = total[part:].astype(BF16)
    across = jnp.where(lax.axis_index("c") == 0, 1.0, 0.0) * tail_of(far_one, embed)
    tail = own[0:1, embed:] + tail_of(near_one, embed)[0:1] + across[0:1]
    out[:, embed:] = split_tail(tail, NC * part)
    sender.send(out, outs[0])


def chip_sum_kernel(own, one, two, *refs):
    keep, send = refs[-2], refs[-1]
    part, embed = own.shape[0], own.shape[1] - LANES
    total = one[:, :embed].astype(F32) + two[:, :embed].astype(F32)
    tail = tail_of(one, embed) + tail_of(two, embed)
    send[:, :embed] = total[part:]
    send[:, embed:] = jnp.zeros((part, LANES), F32)
    send[0:8, embed:] = jnp.broadcast_to(tail, (8, LANES))
    keep[:, :embed] = own[:, :embed] + total[:part]
    keep[:, embed:] = own[:, embed:]
    keep[0:8, embed:] = tail + own[0:8, embed:]


def image_sum_kernel(scale, keep, received, others, out, temp):
    embed = out.shape[1]
    out[...] = keep[:, :embed] + received[:, :embed]
    total = keep[0:8, embed:] + received[0:8, embed:] + others[...]
    temp[...] = total[0:1, 0:1] * scale[0]


def text_sum_kernel(got, unread, out, rows_total):
    part = out.shape[0]
    total = got[0].astype(F32)
    for p in range(1, got.shape[0]):
        total = total + got[p].astype(F32)
    for i in range(out.shape[1] // LANES):
        out[:, i * LANES : (i + 1) * LANES] = total[i * part : (i + 1) * part]
    tail = total[out.shape[1] // LANES * part :][0:8]
    lane = lax.broadcasted_iota(jnp.int32, tail.shape, 1)
    tail = jnp.sum(jnp.where(lane < 3, tail, 0.0), axis=1, keepdims=True)
    rows_total[...] = jnp.broadcast_to(tail, rows_total.shape)


def local(image_embed, text_embed, pair_col, log_scale):
    part, embed = image_embed.shape
    peers = NY * NX
    nz = lax.axis_size("z")
    half = nz * part
    rows, cols = NC * half, peers * part
    count = rows // LANES
    batch = peers * rows
    c = lax.axis_index("c")
    z = lax.axis_index("z")
    scale = jnp.exp(log_scale)
    scale1 = scale[None]
    sds = jax.ShapeDtypeStruct
    vmem = pltpu.VMEM
    last = nz // 2

    def swap(x):
        return lax.ppermute(x, "c", SWAP)

    def ahead(x, k):
        pairs = [((i + k) % nz, i) for i in range(nz)]
        return lax.ppermute(x, CZ, pairs + [(nz + i, nz + (i + k) % nz) for i in range(nz)])

    def onward(x, k):
        pairs = [(i, (i + k) % nz) for i in range(nz)]
        return lax.ppermute(x, CZ, pairs + [(nz + (i + k) % nz, nz + i) for i in range(nz)])

    spread = call(spread_kernel, sds((peers, part, embed), BF16), text_embed, flops=1 << 34, held=(sds((8, LANES), BF16),))
    txt = lax.all_to_all(spread, XY, 0, 0).reshape(cols, embed)
    partner = swap(image_embed)
    chip = jnp.concatenate([image_embed, partner])
    got = [ahead(chip, 1), ahead(chip, 2)]
    got += [ahead(got[1], 1), ahead(got[1][:part], 2)]
    images = got + [image_embed] + [swap(x) for x in got] + [partner]

    rem = pair_col % (cols * NC)
    block = rem // part
    ours = pair_col // (cols * NC) == z
    chip = block // NC
    bits = len(CHIP) - 1
    spot = sum((chip >> (bits - CHIP.index(a)) & 1) << (bits - i) for i, a in enumerate(XY))
    place = (spot * part + rem % part).astype(F32)
    mine = jnp.where(ours & (block % NC == c), place, -1.0)
    theirs = swap(jnp.where(ours & (block % NC == 1 - c), place, -1.0))
    pairs = jnp.where(c == 0, jnp.concatenate([mine, theirs]), jnp.concatenate([theirs, mine]))
    pairs = jnp.pad(pairs, (0, 8 * LANES - rows)).reshape(8, LANES)

    work = 2 * rows * cols * embed
    tile, pad = sds((24, LANES), F32), sds((8, LANES), F32)
    message = sds((MESSAGE, LANES), F32)
    logits, stat, msg = call(
        functools.partial(logits_kernel, nz),
        (sds((rows, cols), F32), tile, sds((peers, MESSAGE, LANES), F32)),
        scale1,
        pairs,
        txt,
        *images,
        flops=work,
        smem=(0,),
        cuts={2: (0, 256)},
        joined=3,
        later=(2, 3),
        held=(None, None, message),
        spare=1 << 20,
        sends=1 + cols // 256 + peers,
        scratch=[vmem((rows, 8), F32), vmem((rows, LANES), F32)],
    )
    col_got = lax.all_to_all(msg, XY, 0, 0)
    chip_stat = jnp.concatenate(merge([stat, swap(stat)]))
    stats = [ahead(chip_stat, k) for k in range(last, 0, -1)]
    merged = jnp.concatenate(merge(stats[1:]))

    wide = embed + LANES
    high = embed // LANES * part + 16
    text_term, first, row_loss, col_loss, sums, send = call(
        functools.partial(grad_kernel, count, nz),
        (sds((peers, high, LANES), BF16), sds((half, cols), BF16), pad, pad, pad, sds((half, wide), BF16)),
        scale1,
        col_got,
        chip_stat,
        stats[0],
        merged,
        swap(merged),
        pairs,
        logits,
        txt,
        *images,
        flops=2 * work,
        smem=(0,),
        cuts={7: (0, part), 8: (1, 256)},
        joined=9,
        later=(8, 9),
        spare=1 << 20,
        scratch=[vmem((rows, 8), F32), vmem((rows, cols), BF16), vmem((cols, rows), BF16)],
    )
    received = swap(send)
    text_got = lax.all_to_all(text_term, XY, 0, 0)
    chip_rows = sds((NC * part, wide), BF16)
    one, two, three, four, own = call(
        image_kernel,
        (chip_rows, sds((NC * part, wide), F32), chip_rows, sds((part, wide), BF16), sds((part, wide), F32)),
        sums,
        first,
        txt,
        received,
        flops=work // 2,
        cuts={2: (1, 256), 3: (1, 256)},
        fixed=(1, 2, 3),
        spare=VMEM_BYTES // 2,
    )
    two = call(forward_kernel, chip_rows, two, onward(three, 1), onward(four, 2), spare=VMEM_BYTES // 2)
    row_loss = lax.dynamic_slice(row_loss, (c * (count // NC), 0), (count // NC, LANES)).reshape(-1)
    col_loss = col_loss[:count].reshape(2, 2, 2, 2, part)
    col_loss = col_loss.transpose([XY.index(a) for a in CHIP] + [4]).reshape(peers, 1, part)
    other = swap(col_loss)
    col_loss = jnp.where(
        c == 0, jnp.concatenate([col_loss, other], 1), jnp.concatenate([other, col_loss], 1)
    ).reshape(-1)
    keep, send = small(
        chip_sum_kernel,
        (sds((part, wide), F32), sds((part, wide), F32)),
        own,
        onward(one, 1),
        onward(two, 2),
        row_loss,
        col_loss,
        unread=(3, 4),
    )
    grad_text, row_total = small(text_sum_kernel, (sds((part, embed), F32), pad), text_got, send, unread=(1,))
    grad_image, temp = small(
        image_sum_kernel,
        (sds((part, embed), F32), sds((1, 1), F32)),
        jnp.full((1,), 1.0 / batch, F32),
        keep,
        swap(send),
        row_total,
        smem=(0,),
    )
    return (row_loss, col_loss, grad_image, grad_text, temp[0, 0])


def solution(mesh):
    nz = mesh.shape["txt"]
    grid = Mesh(mesh.devices.reshape(2, 2, 2, 2, NC, nz), (*CHIP, "c", "z"))
    images, texts = (*CHIP, "c", "z"), ("z", *CHIP, "c")
    in_specs = (P(images, None), P(texts, None), P((*CHIP, "c")), P())
    out_specs = (P((*CHIP, "c")), P("z"), P(images, None), P(texts, None), P())
    return jax.shard_map(local, mesh=grid, in_specs=in_specs, out_specs=out_specs, check_vma=False)
```
